512 devices in a mesh: member: 32 (over z_lo, x, core), band: 16 (over z_hi, y).
Axes of the slice: x: 4, y: 4, z: 16 (z_hi: 4, z_lo: 4; z = z_hi * 4 + z_lo), core: 2. Of those that a mesh axis runs over, the one named last changes fastest.
Arguments:
- controls: float32 [64, 16, 256, 512], P('member', None, 'band'), may hold values from -6 to 6
- members: float32 [64, 16, 256, 512], P('member', None, 'band'), may hold values from -6 to 6
- loc_lon: float32 [512, 512], replicated, may hold values from -0.25 to 0.25
- loc_lat: float32 [256, 256], replicated, may hold values from -0.375 to 0.375
- balance: float32 [5, 1024, 2048], P(None, 'band', 'member'), may hold values from -1 to 1
- innovation: float32 [16, 1024, 2048], P(None, 'band', 'member'), may hold values from -6 to 6
- obs_weight: float32 [16, 1024, 2048], P(None, 'band', 'member'), may hold values from 0.2 to 5
Outputs:
- gradient: float32 [64, 16, 256, 512], P('member', None, 'band')
The draws below stay inside these ranges and needn't reach their ends.
All inputs are finite; a program needn't handle non-finite values.
Results may differ from the reference program's by a relative error of at most 0.00012.
Values sent between devices are 32-bit elements; how exact they have to be, the bound alone decides.
A program may use at most 64 MiB of HBM per device.

```python
import math
import jax
import jax.numpy as jnp
from jax import lax

LEVELS = 16
NYC = 256
NXC = 512
KEN = 64
NYF = 1024
NXF = 2048


def level_of(rng, dims, shards, smallest, high):
    def one(axis_at, shards_of):
        steps = jax.random.uniform(jax.random.fold_in(jax.random.fold_in(rng, 6), axis_at), (shards_of,), jnp.float32, smallest / len(shards), high / len(shards))
        return jnp.repeat(jnp.exp(steps), dims[axis_at] // shards_of).reshape((-1,) + (1,) * (len(dims) - axis_at - 1))

    loudness = one(*shards[0])
    for cut in shards[1:]:
        loudness = loudness * one(*cut)
    return loudness


def normal_values(key, shape, deviation, bound, cuts=(), kind=jnp.bfloat16):
    drawn = deviation * jax.random.normal(key, shape, jnp.float32)
    if cuts:
        drawn = drawn * level_of(key, shape, cuts, -0.22, 0.18)
    return jnp.clip(drawn, -bound, bound).astype(kind)


def setup_inputs(seed: int = 0) -> dict:
    arg_keys = jax.random.split(jax.random.key(seed), 8)
    controls = normal_values(arg_keys[0], (KEN, LEVELS, NYC, NXC), 1.0, 6.0, ((0, 32), (2, 16)), jnp.float32)
    members = normal_values(arg_keys[1], (KEN, LEVELS, NYC, NXC), 1.0, 6.0, ((0, 32), (2, 16)), jnp.float32)
    loc_lon = normal_values(arg_keys[2], (NXC, NXC), NXC ** -0.5, 0.25, (), jnp.float32)
    loc_lat = normal_values(arg_keys[3], (NYC, NYC), NYC ** -0.5, 0.375, (), jnp.float32)
    balance = jnp.clip(jax.random.uniform(arg_keys[4], (5, NYF, NXF), jnp.float32, -1.0, 1.0) * level_of(arg_keys[4], (5, NYF, NXF), ((1, 16), (2, 32)), -0.4, 0.0), -1.0, 1.0)
    innovation = normal_values(arg_keys[5], (LEVELS, NYF, NXF), 1.0, 6.0, ((1, 16), (2, 32)), jnp.float32)
    obs_weight = jnp.clip(jnp.exp(math.log(5.0) - 3.218876 * jax.random.uniform(arg_keys[6], (LEVELS, NYF, NXF), jnp.float32) ** level_of(arg_keys[6], (LEVELS, NYF, NXF), ((1, 16), (2, 32)), -0.2, 0.2)), 0.2, 5.0)
    return {"controls": controls, "members": members, "loc_lon": loc_lon, "loc_lat": loc_lat, "balance": balance, "innovation": innovation, "obs_weight": obs_weight}


phase_fraction = (0.625, 0.875, 0.125, 0.375)
phase_start = (0, 0, 1, 1)

def cubic_weights(fraction):
    return ((-fraction ** 3 + 2 * fraction ** 2 - fraction) / 2, (3 * fraction ** 3 - 5 * fraction ** 2 + 2) / 2, (-3 * fraction ** 3 + 4 * fraction ** 2 + fraction) / 2, (fraction ** 3 - fraction ** 2) / 2)

def refine(padded, dim_index):
    length = padded.shape[dim_index] - 4
    phase_rows = []
    for phase_index in range(4):
        weights = cubic_weights(phase_fraction[phase_index])
        summed = jnp.zeros_like(lax.slice_in_dim(padded, 0, length, axis=dim_index))
        for tap_index in range(4):
            first = phase_start[phase_index] + tap_index
            summed = summed + weights[tap_index] * lax.slice_in_dim(padded, first, first + length, axis=dim_index)
        phase_rows.append(summed)
    stacked = jnp.stack(phase_rows, axis=dim_index + 1)
    new_shape = list(padded.shape)
    new_shape[dim_index] = 4 * length
    return stacked.reshape(new_shape)

def refine_both(padded):
    return refine(refine(padded, 1), 2)

def apply_balance(fine_field, balance):
    grown_field = jnp.pad(fine_field, ((0, 0), (1, 1), (0, 0)))
    grown_field = jnp.concatenate([grown_field[:, :, -1:], grown_field, grown_field[:, :, :1]], axis=2)
    return balance[0] * fine_field + balance[1] * grown_field[:, 1:-1, 2:] + balance[2] * grown_field[:, 1:-1, :-2] + balance[3] * grown_field[:, 2:, 1:-1] + balance[4] * grown_field[:, :-2, 1:-1]

def reference(controls, members, loc_lon, loc_lat, balance, innovation, obs_weight):
    highest = lax.Precision.HIGHEST
    member_scale = 1.0 / math.sqrt(controls.shape[0] - 1)
    rowwise = jnp.einsum('klyx,ux->klyu', controls, loc_lon, precision=highest)
    fields = jnp.einsum('vy,klyx->klvx', loc_lat, rowwise, precision=highest)
    increment = lax.optimization_barrier(jnp.sum(members * fields, axis=0)) * member_scale

    def obs_cost(coarse):
        padded = jnp.pad(coarse, ((0, 0), (2, 2), (0, 0)))
        padded = jnp.concatenate([padded[:, :, -2:], padded, padded[:, :, :2]], axis=2)
        image = apply_balance(refine_both(padded), balance)
        misfit = image - innovation
        return 0.5 * jnp.sum(obs_weight * misfit * misfit)
    coarse_grad = jax.grad(obs_cost)(increment)
    weighted = members * coarse_grad[None] * member_scale
    adjoint = jnp.einsum('klyu,ux->klyx', weighted, loc_lon, precision=highest)
    adjoint = jnp.einsum('vy,klvx->klyx', loc_lat, adjoint, precision=highest)
    return controls + adjoint
```

```python
import math

import jax
import jax.numpy as jnp
import numpy as np
from jax import lax
from jax.experimental import pallas as pl
from jax.experimental.pallas import tpu as pltpu
from jax.sharding import PartitionSpec as P

MESH = pl.DeviceIdType.MESH
BF16 = jnp.bfloat16
F32 = jnp.float32

phase_fraction = (0.625, 0.875, 0.125, 0.375)

KEN, LEVELS, NYC, NXC = 64, 16, 256, 512
BANDS, MEMBERS, XC, ZL = 16, 32, 8, 4
CHUNKS = 2
LC = LEVELS // CHUNKS
LAT, LON = NYC // BANDS, NXC // MEMBERS
SCALE = 1.0 / math.sqrt(KEN - 1)


def cubic_weights(fraction):
    return (
        (-(fraction**3) + 2 * fraction**2 - fraction) / 2,
        (3 * fraction**3 - 5 * fraction**2 + 2) / 2,
        (-3 * fraction**3 + 4 * fraction**2 + fraction) / 2,
        (fraction**3 - fraction**2) / 2,
    )


def refine_rows(shift):
    w = np.zeros((64, 32), np.float32)
    for f in range(64):
        j, r = divmod(f + shift, 4)
        for tap, weight in enumerate(cubic_weights(phase_fraction[r])):
            w[f, j - 2 + tap + (r >= 2) + 8] += weight
    return w


def split_np(w):
    hi = w.astype(BF16)
    lo = (w - hi.astype(np.float32)).astype(BF16)
    return hi, lo


def constants():
    centre, ahead, behind = (refine_rows(s) for s in (0, 1, -1))
    lon = np.zeros((128, 12 * 128), np.float32)
    for s, w in enumerate((centre, ahead, behind)):
        for j in range(4):
            lon[32 * j : 32 * j + 32, (4 * s + j) * 128 : (4 * s + j) * 128 + 64] = w.T
    lh, ll = split_np(lon)
    lon3 = np.concatenate([lh, lh, ll], axis=0)
    th, tl = split_np(np.ascontiguousarray(lon.T))
    lont = np.stack([th, tl])
    lat = np.concatenate([centre, ahead, behind], axis=0)
    ah, al = split_np(lat)
    lat3 = np.concatenate([ah, al, ah], axis=1)
    bh, bl = split_np(np.ascontiguousarray(lat.T))
    latt3 = np.concatenate([bh, bl, bh], axis=1)
    ch, cl = split_np(np.ascontiguousarray(centre.T))
    lattc3 = np.concatenate([ch, cl, ch], axis=1)
    sel = np.zeros((512, 256), np.float32)
    for b in range(BANDS):
        for t in range(32):
            y = 16 * b - 8 + t
            if 0 <= y < NYC:
                sel[32 * b + t, y] = 1
    fold = np.zeros((32, 128), np.float32)
    for j in range(4):
        fold[np.arange(32), 32 * j + np.arange(32)] = 1
    return tuple(
        jnp.asarray(v, BF16)
        for v in (lon3, lont, lat3, latt3, lattc3, sel, np.ascontiguousarray(sel.T), fold)
    )


def split(x):
    hi = x.astype(BF16)
    return hi, (x - hi.astype(F32)).astype(BF16)


def dot(a, b):
    return jnp.dot(a, b, preferred_element_type=F32)


def dot_t(a, b):
    return lax.dot_general(a, b, (((1,), (1,)), ((), ())), preferred_element_type=F32)


def kernel(
    c_ref, m_ref, lonm_ref, latm_ref, bal_ref, inn_ref, ow_ref,
    lon3, lont, lat3, latt3, lattc3, sel, selt, fold,
    out,
    gc, gm, gmt, pt, pa, pbs, pb, sw, z2, r2, ysc, c3, r3, ct, hl, g4, cgt, gb,
    bh, bl, ah, al, bth, btl, ath, atl, bal, inn, ow,
    send, recv, local,
):
    me_m, me_b = lax.axis_index("member"), lax.axis_index("band")
    zl, xc = me_m // XC, me_m % XC

    def band_peer(d):
        return lax.rem(me_b + d, BANDS)

    def on_band(b):
        return {"member": me_m, "band": b}

    def on_member(m):
        return {"member": m, "band": me_b}

    def xc_peer(d):
        return zl * XC + lax.rem(xc + d, XC)

    def zl_peer(d):
        return lax.rem(zl + d, ZL) * XC + xc

    east, west = lax.rem(me_m + 1, MEMBERS), lax.rem(me_m + MEMBERS - 1, MEMBERS)

    barrier = pltpu.get_barrier_semaphore()

    def greet(device):
        pl.semaphore_signal(barrier, inc=1, device_id=device, device_id_type=MESH)

    @pl.loop(1, BANDS)
    def _(d):
        greet(on_band(band_peer(d)))

    @pl.loop(1, XC)
    def _(d):
        greet(on_member(xc_peer(d)))

    @pl.loop(1, ZL)
    def _(d):
        greet(on_member(zl_peer(d)))

    greet(on_member(east))
    greet(on_member(west))
    pl.semaphore_wait(barrier, BANDS - 1 + XC - 1 + ZL - 1 + 2)

    def push(src, dst, ch, ph, device):
        pltpu.make_async_remote_copy(
            src_ref=src, dst_ref=dst, send_sem=send.at[ch, ph], recv_sem=recv.at[ch, ph],
            device_id=device, device_id_type=MESH,
        ).start()

    def wait_for(ref, sem):
        pltpu.make_async_copy(ref, ref, sem).wait()

    def bulk(ch):
        rows = pl.ds(pl.multiple_of(LAT * me_b, LAT), LAT)
        for src, dst, ph in ((c_ref, gc, 0), (m_ref, gm, 1)):

            @pl.loop(1, BANDS)
            def _(d):
                b = band_peer(d)
                push(src.at[lax.rem(b, 2), ch * LC + b // 2], dst.at[ch, rows], ch, ph, on_band(b))

            pltpu.make_async_copy(
                src.at[lax.rem(me_b, 2), ch * LC + me_b // 2], dst.at[ch, rows], local.at[ch, ph]
            ).start()

    def bulk_sent(ch):
        for src, ph in ((gc, 0), (gm, 1)):
            wait_for(src.at[ch, pl.ds(0, 15 * LAT)], send.at[ch, ph])

    def bulk_here(ch, ph):
        src = (gc, gm)[ph]
        wait_for(src.at[ch, pl.ds(0, 15 * LAT)], recv.at[ch, ph])
        wait_for(src.at[ch, pl.ds(0, LAT)], local.at[ch, ph])

    def prepare():
        for ref, hi, lo, thi, tlo in ((lonm_ref, bh, bl, bth, btl), (latm_ref, ah, al, ath, atl)):
            n = ref.shape[0]
            for i in range(n // 128):
                w = ref[pl.ds(128 * i, 128), :]
                h, l = split(w)
                hi[pl.ds(128 * i, 128), :] = h
                lo[pl.ds(128 * i, 128), :] = l
                h, l = split(w.T)
                thi[:, pl.ds(128 * i, 128)] = h
                tlo[:, pl.ds(128 * i, 128)] = l
        for src, dst in ((bal_ref, bal), (inn_ref, inn), (ow_ref, ow)):
            dst[...] = jnp.zeros_like(dst)
            dst[:, :, pl.ds(0, 64)] = src[...]
        row = lax.broadcasted_iota(jnp.int32, (64, 128), 0)
        bal[3] = jnp.where((row == 63) & (me_b == BANDS - 1), 0.0, bal[3])
        bal[4] = jnp.where((row == 0) & (me_b == 0), 0.0, bal[4])

    def fields(ch):
        bulk_here(ch, 0)
        bulk_here(ch, 1)
        for i in range(4):
            gmt[ch, pl.ds(128 * i, 128), :] = gm[ch, :, pl.ds(128 * i, 128)].T
        chh, chl = split(gc[ch])

        @pl.loop(0, 4)
        def _(i):
            rows = pl.ds(pl.multiple_of(128 * i, 128), 128)
            x = dot_t(bh[rows, :], chh) + dot_t(bh[rows, :], chl) + dot_t(bl[rows, :], chh)
            xh, xl = split(x)
            f = dot_t(xh, ah[...]) + dot_t(xl, ah[...]) + dot_t(xh, al[...])
            pt[ch, i] = (f * gmt[ch, rows, :] * SCALE).reshape(XC, LON, NYC)

        @pl.loop(1, XC)
        def _(d):
            p = xc_peer(d)
            push(pt.at[ch, :, lax.rem(p, XC)], pa.at[ch, xc], ch, 2, on_member(p))

        pa[ch, xc] = pt[ch, :, xc]

    def reduce_b(ch):
        wait_for(pa.at[ch, pl.ds(0, XC - 1)], recv.at[ch, 2])
        total = pa[ch, 0]
        for i in range(1, XC):
            total = total + pa[ch, i]
        pbs[ch] = total

        @pl.loop(1, ZL)
        def _(d):
            p = zl_peer(d)
            push(pbs.at[ch, p // XC], pb.at[ch, zl], ch, 3, on_member(p))

        pb[ch, zl] = pbs[ch, zl]

    def halo(ch):
        wait_for(pb.at[ch, pl.ds(0, ZL - 1)], recv.at[ch, 3])
        sw[ch, pl.ds(8, LON)] = pb[ch, 0] + pb[ch, 1] + pb[ch, 2] + pb[ch, 3]
        push(sw.at[ch, pl.ds(8, 8)], sw.at[ch, pl.ds(24, 8)], ch, 4, on_member(west))
        push(sw.at[ch, pl.ds(16, 8)], sw.at[ch, pl.ds(0, 8)], ch, 5, on_member(east))

    def hand_out(ch):
        wait_for(sw.at[ch, pl.ds(24, 8)], recv.at[ch, 4])
        wait_for(sw.at[ch, pl.ds(0, 8)], recv.at[ch, 5])
        w = sw[ch]
        wh, wl = split(jnp.concatenate([w, w, w, w], axis=0))
        z = (dot_t(sel[...], wh) + dot_t(sel[...], wl)).reshape(BANDS, 4, 8, 128)
        group = lax.broadcasted_iota(jnp.int32, (BANDS, 8, 128), 2) // 32
        packed = z[:, 0]
        for j in range(1, 4):
            packed = jnp.where(group == j, z[:, j], packed)
        z2[ch] = packed

        @pl.loop(1, BANDS)
        def _(d):
            b = band_peer(d)
            push(z2.at[ch, b], r2.at[ch, me_b], ch, 6, on_band(b))

        r2[ch, me_b] = z2[ch, me_b]

    def fine(ch):
        wait_for(r2.at[ch, pl.ds(0, BANDS - 1)], recv.at[ch, 6])
        x = r2[ch].reshape(LC, 2, 8, 128)
        xh, xl = split((x[:, 0] + x[:, 1]).reshape(LC * 8, 128))
        y = dot(jnp.concatenate([xh, xl, xh], axis=1), lon3[...])
        for s in range(3):
            for j in range(4):
                for lev in range(LC):
                    ysc[s, pl.ds(8 * j, 8), pl.ds(128 * lev, 128)] = y[
                        8 * lev : 8 * lev + 8, (4 * s + j) * 128 : (4 * s + j + 1) * 128
                    ]

        def stacked(v):
            h, l = split(v)
            return jnp.concatenate([h, h, l], axis=0)

        v_c = dot(lat3[...], stacked(ysc[0]))
        v_e = dot(lat3[pl.ds(0, 64), :], stacked(ysc[1]))
        v_w = dot(lat3[pl.ds(0, 64), :], stacked(ysc[2]))
        to_c, to_e, to_w = [], [], []
        for lev in range(LC):
            at = slice(128 * lev, 128 * lev + 128)
            image = (
                bal[0] * v_c[0:64, at] + bal[1] * v_e[:, at] + bal[2] * v_w[:, at]
                + bal[3] * v_c[64:128, at] + bal[4] * v_c[128:192, at]
            )
            misfit = ow[ch * LC + lev] * (image - inn[ch * LC + lev])
            to_c.append(
                jnp.concatenate([bal[0] * misfit, bal[3] * misfit, bal[4] * misfit], axis=0)
            )
            to_e.append(bal[1] * misfit)
            to_w.append(bal[2] * misfit)
        t = (
            dot(latt3[...], stacked(jnp.concatenate(to_c, axis=1))),
            dot(lattc3[...], stacked(jnp.concatenate(to_e, axis=1))),
            dot(lattc3[...], stacked(jnp.concatenate(to_w, axis=1))),
        )
        rows = []
        for lev in range(LC):
            rows.append(
                jnp.concatenate(
                    [
                        t[s][8 * j : 8 * j + 8, 128 * lev : 128 * lev + 128]
                        for s in range(3)
                        for j in range(4)
                    ],
                    axis=1,
                )
            )
        lh, ll = split(jnp.concatenate(rows, axis=0))
        c3[ch] = (dot(lh, lont[0]) + dot(ll, lont[0]) + dot(lh, lont[1])).reshape(LC, 8, 128)

        @pl.loop(1, BANDS)
        def _(d):
            b = band_peer(d)
            push(c3.at[ch, b // 2], r3.at[ch, me_b], ch, 7, on_band(b))

        r3[ch, me_b] = c3[ch, me_b // 2]

    def gather_in(ch):
        wait_for(r3.at[ch, pl.ds(0, BANDS - 1)], recv.at[ch, 7])
        group = lax.broadcasted_iota(jnp.int32, (BANDS, 8, 128), 2) // 32
        r = r3[ch]
        e = jnp.stack([jnp.where(group == j, r, 0.0) for j in range(4)], axis=1)
        eh, el = split(e.reshape(512, 128))
        oh, ol = split(dot(selt[...], eh) + dot(selt[...], el))
        ct[ch] = dot_t(fold[...], oh) + dot_t(fold[...], ol)
        push(ct.at[ch, pl.ds(0, 8)], hl.at[ch, 1], ch, 8, on_member(west))
        push(ct.at[ch, pl.ds(24, 8)], hl.at[ch, 0], ch, 9, on_member(east))

    def spread_b(ch):
        wait_for(hl.at[ch, 1], recv.at[ch, 8])
        wait_for(hl.at[ch, 0], recv.at[ch, 9])
        own = ct[ch, pl.ds(8, LON)] + jnp.concatenate([hl[ch, 0], hl[ch, 1]], axis=0)
        g4[ch, zl] = own * SCALE

        @pl.loop(1, ZL)
        def _(d):
            push(g4.at[ch, zl], g4.at[ch, zl], ch, 10, on_member(zl_peer(d)))

    def spread_a(ch):
        wait_for(g4.at[ch, pl.ds(0, ZL - 1)], recv.at[ch, 10])

        @pl.loop(1, XC)
        def _(d):
            push(g4.at[ch], cgt.at[ch, :, xc], ch, 11, on_member(xc_peer(d)))

        cgt[ch, :, xc] = g4[ch]

    def adjoint(ch):
        wait_for(cgt.at[ch, :, pl.ds(0, XC - 1)], recv.at[ch, 11])
        wh, wl = split(gmt[ch] * cgt[ch].reshape(NXC, NYC))
        for i in range(4):
            rows = pl.ds(128 * i, 128)
            h = dot(bth[rows, :], wh) + dot(bth[rows, :], wl) + dot(btl[rows, :], wh)
            hh, hlo = split(h)
            gb[ch, :, rows] = dot_t(ath[...], hh) + dot_t(ath[...], hlo) + dot_t(atl[...], hh)
        k, lev = lax.rem(me_b, 2), ch * LC + me_b // 2

        @pl.loop(1, BANDS)
        def _(d):
            b = band_peer(d)
            rows = pl.ds(pl.multiple_of(LAT * b, LAT), LAT)
            push(gb.at[ch, rows], out.at[k, lev], ch, 12, on_band(b))

        out[k, lev] = gb[ch, pl.ds(pl.multiple_of(LAT * me_b, LAT), LAT), :]

    def finish(ch):
        wait_for(gb.at[ch, pl.ds(0, 15 * LAT)], recv.at[ch, 12])
        wait_for(pa.at[ch, pl.ds(0, XC - 1)], send.at[ch, 2])
        wait_for(pb.at[ch, pl.ds(0, ZL - 1)], send.at[ch, 3])
        wait_for(sw.at[ch, pl.ds(0, 8)], send.at[ch, 4])
        wait_for(sw.at[ch, pl.ds(0, 8)], send.at[ch, 5])
        wait_for(r2.at[ch, pl.ds(0, BANDS - 1)], send.at[ch, 6])
        wait_for(r3.at[ch, pl.ds(0, BANDS - 1)], send.at[ch, 7])
        wait_for(hl.at[ch, 1], send.at[ch, 8])
        wait_for(hl.at[ch, 0], send.at[ch, 9])
        wait_for(pb.at[ch, pl.ds(0, ZL - 1)], send.at[ch, 10])
        wait_for(pa.at[ch, pl.ds(0, XC - 1)], send.at[ch, 11])
        wait_for(gb.at[ch, pl.ds(0, 15 * LAT)], send.at[ch, 12])

    bulk(0)
    prepare()
    bulk_sent(0)
    bulk(1)
    for stage in (fields, reduce_b, halo, hand_out, fine, gather_in, spread_b, spread_a, adjoint):
        stage(0)
    for stage in (fields, reduce_b, halo, hand_out, fine, gather_in, spread_b, spread_a, adjoint):
        stage(1)
    bulk_sent(1)
    finish(0)
    finish(1)


def body(controls, members, loc_lon, loc_lat, balance, innovation, obs_weight):
    consts = constants()
    vmem = pl.BlockSpec(memory_space=pltpu.VMEM)
    f32 = lambda *s: pltpu.VMEM(s, F32)
    b16 = lambda *s: pltpu.VMEM(s, BF16)
    adjoint = pl.pallas_call(
        kernel,
        out_shape=jax.ShapeDtypeStruct(controls.shape, F32),
        in_specs=[vmem] * (7 + len(consts)),
        out_specs=vmem,
        scratch_shapes=[
            f32(CHUNKS, NYC, NXC),
            f32(CHUNKS, NYC, NXC),
            f32(CHUNKS, NXC, NYC),
            f32(CHUNKS, ZL, XC, LON, NYC),
            f32(CHUNKS, XC, ZL, LON, NYC),
            f32(CHUNKS, ZL, LON, NYC),
            f32(CHUNKS, ZL, LON, NYC),
            f32(CHUNKS, 32, NYC),
            f32(CHUNKS, BANDS, 8, 128),
            f32(CHUNKS, BANDS, 8, 128),
            f32(3, 32, LC * 128),
            f32(CHUNKS, LC, 8, 128),
            f32(CHUNKS, BANDS, 8, 128),
            f32(CHUNKS, 32, NYC),
            f32(CHUNKS, 2, 8, NYC),
            f32(CHUNKS, ZL, LON, NYC),
            f32(CHUNKS, ZL, XC, LON, NYC),
            f32(CHUNKS, NYC, NXC),
            b16(NXC, NXC), b16(NXC, NXC), b16(NYC, NYC), b16(NYC, NYC),
            b16(NXC, NXC), b16(NXC, NXC), b16(NYC, NYC), b16(NYC, NYC),
            f32(5, 64, 128), f32(LEVELS, 64, 128), f32(LEVELS, 64, 128),
            pltpu.SemaphoreType.DMA((CHUNKS, 13)),
            pltpu.SemaphoreType.DMA((CHUNKS, 13)),
            pltpu.SemaphoreType.DMA((CHUNKS, 2)),
        ],
        compiler_params=pltpu.CompilerParams(
            collective_id=0, has_side_effects=True, vmem_limit_bytes=56 << 20
        ),
        name="gradient",
    )(controls, members, loc_lon, loc_lat, balance, innovation, obs_weight, *consts)
    return controls + adjoint


def solution(mesh):
    return jax.shard_map(
        body,
        mesh=mesh,
        in_specs=(
            P("member", None, "band", None),
            P("member", None, "band", None),
            P(),
            P(),
            P(None, "band", "member"),
            P(None, "band", "member"),
            P(None, "band", "member"),
        ),
        out_specs=P("member", None, "band", None),
        check_vma=False,
    )
```

```python
import math

import jax
import jax.numpy as jnp
import numpy as np
from jax import lax
from jax.experimental import pallas as pl
from jax.experimental.pallas import tpu as pltpu
from jax.sharding import PartitionSpec as P

MESH = pl.DeviceIdType.MESH
BF16 = jnp.bfloat16
F32 = jnp.float32

phase_fraction = (0.625, 0.875, 0.125, 0.375)

KEN, LEVELS, NYC, NXC = 64, 16, 256, 512
BANDS, MEMBERS, XC, ZL = 16, 32, 8, 4
ZH, YB = 4, 4
BLOCK = NYC // ZH
LAT, LON = NYC // BANDS, NXC // MEMBERS
SCALE = 1.0 / math.sqrt(KEN - 1)


def cubic_weights(fraction):
    return (
        (-(fraction**3) + 2 * fraction**2 - fraction) / 2,
        (3 * fraction**3 - 5 * fraction**2 + 2) / 2,
        (-3 * fraction**3 + 4 * fraction**2 + fraction) / 2,
        (fraction**3 - fraction**2) / 2,
    )


def refine_rows(shift):
    w = np.zeros((64, 32), np.float32)
    for f in range(64):
        j, r = divmod(f + shift, 4)
        for tap, weight in enumerate(cubic_weights(phase_fraction[r])):
            w[f, j - 2 + tap + (r >= 2) + 8] += weight
    return w


def split_np(w):
    hi = w.astype(BF16)
    lo = (w - hi.astype(np.float32)).astype(BF16)
    return hi, lo


def constants():
    centre, ahead, behind = (refine_rows(s) for s in (0, 1, -1))
    lon = np.zeros((128, 12 * 128), np.float32)
    for s, w in enumerate((centre, ahead, behind)):
        for j in range(4):
            lon[32 * j : 32 * j + 32, (4 * s + j) * 128 : (4 * s + j) * 128 + 64] = w.T
    lh, ll = split_np(lon)
    lon3 = np.concatenate([lh, lh, ll], axis=0)
    th, tl = split_np(np.ascontiguousarray(lon.T))
    lont = np.stack([th, tl])
    lat = np.concatenate([centre, ahead, behind], axis=0)
    ah, al = split_np(lat)
    lat3 = np.concatenate([ah, al, ah], axis=1)
    bh, bl = split_np(np.ascontiguousarray(lat.T))
    latt3 = np.concatenate([bh, bl, bh], axis=1)
    ch, cl = split_np(np.ascontiguousarray(centre.T))
    lattc3 = np.concatenate([ch, cl, ch], axis=1)
    sel = np.zeros((512, 256), np.float32)
    for b in range(BANDS):
        for t in range(32):
            y = 16 * b - 8 + t
            if 0 <= y < NYC:
                sel[32 * b + t, y] = 1
    fold = np.zeros((32, 128), np.float32)
    for j in range(4):
        fold[np.arange(32), 32 * j + np.arange(32)] = 1
    return tuple(
        jnp.asarray(v, BF16)
        for v in (lon3, lont, lat3, latt3, lattc3, sel, np.ascontiguousarray(sel.T), fold)
    )


def split(x):
    hi = x.astype(BF16)
    return hi, (x - hi.astype(F32)).astype(BF16)


def dot(a, b):
    return jnp.dot(a, b, preferred_element_type=F32)


def dot_t(a, b):
    return lax.dot_general(a, b, (((1,), (1,)), ((), ())), preferred_element_type=F32)


def kernel(
    c_hbm, m_hbm, lon_hbm, lat_hbm, bal_hbm, inn_hbm, ow_hbm, *rest
):
    consts_hbm, (
        out,
        lonm, latm, bal_in, inn_in, ow_in,
        lon3, lont, lat3, latt3, lattc3, sel, selt, fold,
        gc, gm, ft, pt, pa, pbs, pb, sw, z2, r2, ysc, c3, r3, ct, hl, g4, cgt, gb, wsc,
        bh, bl, latf, ap3, atph, atpl, bal, inn, ow,
        send, recv, local, loads,
    ) = rest[:8], rest[8:]
    me_m, me_b = lax.axis_index("member"), lax.axis_index("band")
    zl, xc = me_m // XC, me_m % XC
    zh, yb = me_b // YB, me_b % YB
    level = (me_b, lax.rem(me_b + BANDS - YB, BANDS))
    outer = (lax.rem(zh + ZH - 1, ZH), lax.rem(zh + 1, ZH))

    def band_peer(i):
        return lax.rem(me_b + 1 + lax.rem(i + 7, BANDS - 1), BANDS)

    def on_band(b):
        return {"member": me_m, "band": b}

    def on_member(m):
        return {"member": m, "band": me_b}

    def xc_peer(d):
        return zl * XC + lax.rem(xc + d, XC)

    def zl_peer(d):
        return lax.rem(zl + d, ZL) * XC + xc

    east, west = lax.rem(me_m + 1, MEMBERS), lax.rem(me_m + MEMBERS - 1, MEMBERS)

    barrier = pltpu.get_barrier_semaphore()

    def greet(device):
        pl.semaphore_signal(barrier, inc=1, device_id=device, device_id_type=MESH)

    @pl.loop(0, BANDS - 1)
    def _(i):
        greet(on_band(band_peer(i)))

    @pl.loop(1, ZL)
    def _(d):
        greet(on_member(zl_peer(d)))

    @pl.loop(1, XC)
    def _(d):
        greet(on_member(xc_peer(d)))

    greet(on_member(east))
    greet(on_member(west))

    loaded = [
        pltpu.make_async_copy(src, dst, loads.at[n])
        for n, (src, dst) in enumerate(
            zip(
                (lon_hbm, lat_hbm, bal_hbm, inn_hbm, ow_hbm, *consts_hbm),
                (lonm, latm, bal_in, inn_in, ow_in, lon3, lont, lat3, latt3, lattc3, sel, selt, fold),
            )
        )
    ]
    mine = pl.ds(pl.multiple_of(LAT * yb, LAT), LAT)
    mine_all = pl.ds(pl.multiple_of(LAT * me_b, LAT), LAT)
    own = [
        pltpu.make_async_copy(src.at[:, level[s]], dst.at[s, :, rows], local.at[s, n])
        for s in range(2)
        for n, (src, dst, rows) in enumerate(((c_hbm, gc, mine), (m_hbm, gm, mine_all)))
    ]
    for copy in loaded + own:
        copy.start()
    pl.semaphore_wait(barrier, BANDS - 1 + XC - 1 + ZL - 1 + 2)

    def push(src, dst, ph, device):
        pltpu.make_async_remote_copy(
            src_ref=src, dst_ref=dst, send_sem=send.at[ph], recv_sem=recv.at[ph],
            device_id=device, device_id_type=MESH,
        ).start()

    def wait_for(ref, sem):
        pltpu.make_async_copy(ref, ref, sem).wait()

    def level_at(b, slot):
        return b if slot == 0 else lax.rem(b + BANDS - YB, BANDS)

    def send_members(b, slot, ph):
        push(m_hbm.at[:, level_at(b, slot)], gm.at[slot, :, mine_all], ph, on_band(b))

    def send_controls(b, slot, half):
        rows = pl.ds(pl.multiple_of(BLOCK * half + LAT * yb, LAT), LAT)
        push(c_hbm.at[:, level_at(b, slot)], gc.at[slot, :, rows], slot, on_band(b))

    def ahead(y):
        return outer[1] * YB + lax.rem(yb + y, YB)

    def behind(y):
        return outer[0] * YB + lax.rem(yb + y, YB)

    def beside(y):
        return zh * YB + lax.rem(yb + y, YB)

    @pl.loop(0, YB)
    def _(y):
        send_members(ahead(y), 0, 2)
        send_members(behind(y), 1, 3)

    @pl.loop(0, YB)
    def _(y):
        send_controls(ahead(y), 0, 1)
        send_controls(behind(y), 1, 1)

    @pl.loop(1, YB)
    def _(y):
        send_controls(beside(y), 0, 0)
        send_controls(beside(y), 1, 0)

    @pl.loop(0, YB)
    def _(y):
        send_members(behind(y), 0, 4)
        send_members(ahead(y), 1, 5)

    @pl.loop(1, YB)
    def _(y):
        send_members(beside(y), 0, 4)
        send_members(beside(y), 1, 5)

    two = gm.at[0, 0, pl.ds(0, 8 * LAT)]
    seven = gm.at[0, 0, pl.ds(0, 14 * LAT)]

    def block(group):
        return pl.ds(pl.multiple_of(BLOCK * group, BLOCK), BLOCK)

    def relay():
        wait_for(two, recv.at[3])
        rows = block(outer[1])
        push(gm.at[1, :, rows], gm.at[0, :, rows], 6, on_band(outer[0] * YB + yb))
        wait_for(two, recv.at[2])
        rows = block(outer[0])
        push(gm.at[0, :, rows], gm.at[1, :, rows], 7, on_band(outer[1] * YB + yb))

    def prepare():
        for copy in loaded:
            copy.wait()
        for i in range(4):
            rows = pl.ds(128 * i, 128)
            bh[rows, :], bl[rows, :] = split(lonm[rows, :])
        for i in range(2):
            latf[:, pl.ds(128 * i, 128)] = latm[pl.ds(128 * i, 128), :].T
        for s in range(2):
            half = jnp.concatenate([latf[block(zh), :], latf[block(outer[s]), :]], axis=0)
            atph[s], atpl[s] = split(half)
            h, l = split(half.T)
            ap3[s] = jnp.concatenate([h, l, h], axis=1)
        for src, dst in ((bal_in, bal), (inn_in, inn), (ow_in, ow)):
            dst[...] = jnp.zeros_like(dst)
            dst[:, :, pl.ds(0, 64)] = src[...]
        row = lax.broadcasted_iota(jnp.int32, (64, 128), 0)
        bal[3] = jnp.where((row == 63) & (me_b == BANDS - 1), 0.0, bal[3])
        bal[4] = jnp.where((row == 0) & (me_b == 0), 0.0, bal[4])

    def fields():
        for copy in own:
            copy.wait()
        wait_for(seven, recv.at[0])
        wait_for(seven, recv.at[1])

        @pl.loop(0, 2)
        def _(s):
            @pl.loop(0, 2)
            def _(k):
                ch, cl = split(gc[s, k])
                x = dot_t(ch, bh[...]) + dot_t(cl, bh[...]) + dot_t(ch, bl[...])
                xh, xl = split(x)
                ft[s, k] = dot(ap3[s], jnp.concatenate([xh, xh, xl], axis=0))

    def products(s):
        wait_for(seven, recv.at[4 + s])
        wait_for(two, recv.at[6 + s])
        for i in range(ZL):
            at = pl.ds(128 * i, 128)
            p = (gm[s, 0, :, at] * ft[s, 0, :, at] + gm[s, 1, :, at] * ft[s, 1, :, at]) * SCALE
            pt[s, i] = p.T.reshape(XC, LON, NYC)

        @pl.loop(1, XC)
        def _(d):
            p = xc_peer(d)
            push(pt.at[s, :, lax.rem(p, XC)], pa.at[s, xc], 8 + s, on_member(p))

        pa[s, xc] = pt[s, :, xc]

    def reduce_b():
        for s in range(2):
            wait_for(pa.at[s, pl.ds(0, XC - 1)], recv.at[8 + s])
            total = pa[s, 0]
            for i in range(1, XC):
                total = total + pa[s, i]
            pbs[:, s] = total

        @pl.loop(1, ZL)
        def _(d):
            p = zl_peer(d)
            push(pbs.at[p // XC], pb.at[zl], 10, on_member(p))

        pb[zl] = pbs[zl]

    def halo():
        wait_for(pb.at[pl.ds(0, ZL - 1)], recv.at[10])
        sw[:, pl.ds(8, LON)] = pb[0] + pb[1] + pb[2] + pb[3]
        push(sw.at[:, pl.ds(8, 8)], sw.at[:, pl.ds(24, 8)], 11, on_member(west))
        push(sw.at[:, pl.ds(16, 8)], sw.at[:, pl.ds(0, 8)], 12, on_member(east))

    def hand_out():
        wait_for(sw.at[:, pl.ds(24, 8)], recv.at[11])
        wait_for(sw.at[:, pl.ds(0, 8)], recv.at[12])
        w, v = sw[0], sw[1]
        wh, wl = split(jnp.concatenate([w, w, w, w, v, v, v, v], axis=0))
        z = dot_t(sel[...], wh) + dot_t(sel[...], wl)
        group = lax.broadcasted_iota(jnp.int32, (BANDS, 8, 128), 2) // 32
        for s in range(2):
            zs = z[:, 128 * s : 128 * s + 128].reshape(BANDS, 4, 8, 128)
            packed = zs[:, 0]
            for j in range(1, 4):
                packed = jnp.where(group == j, zs[:, j], packed)
            z2[:, s] = packed

        @pl.loop(0, BANDS - 1)
        def _(i):
            b = band_peer(i)
            push(z2.at[b], r2.at[me_b], 13, on_band(b))

        r2[me_b] = z2[me_b]

    def fine():
        wait_for(r2.at[pl.ds(0, BANDS - 1)], recv.at[13])
        x = jnp.concatenate(
            [r2[lev, 0] + r2[(lev + YB) % BANDS, 1] for lev in range(LEVELS)], axis=0
        )
        xh, xl = split(x)
        y = dot(jnp.concatenate([xh, xl, xh], axis=1), lon3[...])
        for s in range(3):
            for j in range(4):
                for lev in range(LEVELS):
                    ysc[s, pl.ds(8 * j, 8), pl.ds(128 * lev, 128)] = y[
                        8 * lev : 8 * lev + 8, (4 * s + j) * 128 : (4 * s + j + 1) * 128
                    ]

        def stacked(v):
            h, l = split(v)
            return jnp.concatenate([h, h, l], axis=0)

        v_c = dot(lat3[...], stacked(ysc[0]))
        v_e = dot(lat3[pl.ds(0, 64), :], stacked(ysc[1]))
        v_w = dot(lat3[pl.ds(0, 64), :], stacked(ysc[2]))
        to_c, to_e, to_w = [], [], []
        for lev in range(LEVELS):
            at = slice(128 * lev, 128 * lev + 128)
            image = (
                bal[0] * v_c[0:64, at] + bal[1] * v_e[:, at] + bal[2] * v_w[:, at]
                + bal[3] * v_c[64:128, at] + bal[4] * v_c[128:192, at]
            )
            misfit = ow[lev] * (image - inn[lev])
            to_c.append(
                jnp.concatenate([bal[0] * misfit, bal[3] * misfit, bal[4] * misfit], axis=0)
            )
            to_e.append(bal[1] * misfit)
            to_w.append(bal[2] * misfit)
        t = (
            dot(latt3[...], stacked(jnp.concatenate(to_c, axis=1))),
            dot(lattc3[...], stacked(jnp.concatenate(to_e, axis=1))),
            dot(lattc3[...], stacked(jnp.concatenate(to_w, axis=1))),
        )
        rows = []
        for lev in range(LEVELS):
            rows.append(
                jnp.concatenate(
                    [
                        t[s][8 * j : 8 * j + 8, 128 * lev : 128 * lev + 128]
                        for s in range(3)
                        for j in range(4)
                    ],
                    axis=1,
                )
            )
        lh, ll = split(jnp.concatenate(rows, axis=0))
        c = dot(lh, lont[0]) + dot(ll, lont[0]) + dot(lh, lont[1])
        for lev in range(LEVELS):
            c3[lev, 0] = c[8 * lev : 8 * lev + 8]
            c3[(lev + YB) % BANDS, 1] = c[8 * lev : 8 * lev + 8]

        @pl.loop(0, BANDS - 1)
        def _(i):
            b = band_peer(i)
            push(c3.at[b], r3.at[me_b], 14, on_band(b))

        r3[me_b] = c3[me_b]

    def gather_in():
        wait_for(r3.at[pl.ds(0, BANDS - 1)], recv.at[14])
        group = lax.broadcasted_iota(jnp.int32, (BANDS, 8, 128), 2) // 32
        both = []
        for s in range(2):
            r = r3[:, s]
            e = jnp.stack([jnp.where(group == j, r, 0.0) for j in range(4)], axis=1)
            both.append(e.reshape(512, 128))
        eh, el = split(jnp.concatenate(both, axis=1))
        oh, ol = split(dot(selt[...], eh) + dot(selt[...], el))
        for s in range(2):
            at = slice(128 * s, 128 * s + 128)
            ct[s] = dot_t(fold[...], oh[:, at]) + dot_t(fold[...], ol[:, at])
        push(ct.at[:, pl.ds(0, 8)], hl.at[1], 15, on_member(west))
        push(ct.at[:, pl.ds(24, 8)], hl.at[0], 16, on_member(east))

    def spread_b():
        wait_for(hl.at[1], recv.at[15])
        wait_for(hl.at[0], recv.at[16])
        own_part = ct[:, pl.ds(8, LON)] + jnp.concatenate([hl[0], hl[1]], axis=1)
        g4[zl] = own_part * SCALE

        @pl.loop(1, ZL)
        def _(d):
            push(g4.at[zl], g4.at[zl], 17, on_member(zl_peer(d)))

    def spread_a():
        wait_for(g4.at[pl.ds(0, ZL - 1)], recv.at[17])
        for s in range(2):

            @pl.loop(1, XC)
            def _(d):
                push(g4.at[:, s], cgt.at[s, :, xc], 18 + s, on_member(xc_peer(d)))

            cgt[s, :, xc] = g4[:, s]

    def adjoint(s):
        wait_for(cgt.at[s, :, pl.ds(0, XC - 1)], recv.at[18 + s])
        for i in range(ZL):
            at = pl.ds(128 * i, 128)
            g = cgt[s, i].reshape(128, NYC).T
            for k in range(2):
                w = gm[s, k, :, at] * g
                h = w.astype(BF16)
                wsc[0, k, :, at] = h
                wsc[1, k, :, at] = (w - h.astype(F32)).astype(BF16)
        for k in range(2):
            t = dot(atph[s], wsc[0, k]) + dot(atpl[s], wsc[0, k]) + dot(atph[s], wsc[1, k])
            th, tl = split(t)
            gb[s, k] = dot(th, bh[...]) + dot(tl, bh[...]) + dot(th, bl[...])

        def give(b, half, y):
            rows = pl.ds(pl.multiple_of(BLOCK * half + LAT * y, LAT), LAT)
            push(gb.at[s, :, rows], out.at[:, level[s]], 20 + s, on_band(b))

        far = (behind, ahead)[s]

        @pl.loop(0, YB)
        def _(y):
            give(far(y), 1, lax.rem(yb + y, YB))

        @pl.loop(1, YB)
        def _(y):
            give(beside(y), 0, lax.rem(yb + y, YB))

        out[:, level[s]] = gb[s, :, mine, :]

    def finish():
        for s in range(2):
            wait_for(seven, recv.at[20 + s])
        for ph in (0, 1, 4, 5, 20, 21):
            wait_for(seven, send.at[ph])
        for ph in (2, 3, 6, 7):
            wait_for(two, send.at[ph])
        for s in range(2):
            wait_for(pa.at[s, pl.ds(0, XC - 1)], send.at[8 + s])
            wait_for(pa.at[s, pl.ds(0, XC - 1)], send.at[18 + s])
        wait_for(pb.at[pl.ds(0, ZL - 1)], send.at[10])
        wait_for(pb.at[pl.ds(0, ZL - 1)], send.at[17])
        wait_for(sw.at[:, pl.ds(24, 8)], send.at[11])
        wait_for(sw.at[:, pl.ds(24, 8)], send.at[12])
        wait_for(r2.at[pl.ds(0, BANDS - 1)], send.at[13])
        wait_for(r3.at[pl.ds(0, BANDS - 1)], send.at[14])
        wait_for(hl.at[1], send.at[15])
        wait_for(hl.at[0], send.at[16])

    relay()
    prepare()
    fields()
    products(0)
    products(1)
    reduce_b()
    halo()
    hand_out()
    fine()
    gather_in()
    spread_b()
    spread_a()
    adjoint(0)
    adjoint(1)
    finish()


def body(controls, members, loc_lon, loc_lat, balance, innovation, obs_weight):
    consts = constants()
    hbm = pl.BlockSpec(memory_space=pl.ANY)
    vmem = pl.BlockSpec(memory_space=pltpu.VMEM)
    f32 = lambda *s: pltpu.VMEM(s, F32)
    b16 = lambda *s: pltpu.VMEM(s, BF16)
    small = (loc_lon, loc_lat, balance, innovation, obs_weight)
    adjoint = pl.pallas_call(
        kernel,
        out_shape=jax.ShapeDtypeStruct(controls.shape, F32),
        in_specs=[hbm] * (7 + len(consts)),
        out_specs=vmem,
        scratch_shapes=[pltpu.VMEM(v.shape, v.dtype) for v in (*small, *consts)]
        + [
            f32(2, 2, 2 * BLOCK, NXC),
            f32(2, 2, NYC, NXC),
            f32(2, 2, NYC, NXC),
            f32(2, ZL, XC, LON, NYC),
            f32(2, XC, ZL, LON, NYC),
            f32(ZL, 2, LON, NYC),
            f32(ZL, 2, LON, NYC),
            f32(2, 32, NYC),
            f32(BANDS, 2, 8, 128),
            f32(BANDS, 2, 8, 128),
            f32(3, 32, LEVELS * 128),
            f32(BANDS, 2, 8, 128),
            f32(BANDS, 2, 8, 128),
            f32(2, 32, NYC),
            f32(2, 2, 8, NYC),
            f32(ZL, 2, LON, NYC),
            f32(2, ZL, XC, LON, NYC),
            f32(2, 2, 2 * BLOCK, NXC),
            b16(2, 2, NYC, NXC),
            b16(NXC, NXC), b16(NXC, NXC), f32(NYC, NYC),
            b16(2, NYC, 6 * BLOCK), b16(2, 2 * BLOCK, NYC), b16(2, 2 * BLOCK, NYC),
            f32(5, 64, 128), f32(LEVELS, 64, 128), f32(LEVELS, 64, 128),
            pltpu.SemaphoreType.DMA((22,)),
            pltpu.SemaphoreType.DMA((22,)),
            pltpu.SemaphoreType.DMA((2, 2)),
            pltpu.SemaphoreType.DMA((13,)),
        ],
        compiler_params=pltpu.CompilerParams(
            collective_id=0, has_side_effects=True, vmem_limit_bytes=56 << 20
        ),
        name="gradient",
    )(controls, members, *small, *consts)
    return controls + adjoint


def solution(mesh):
    return jax.shard_map(
        body,
        mesh=mesh,
        in_specs=(
            P("member", None, "band", None),
            P("member", None, "band", None),
            P(),
            P(),
            P(None, "band", "member"),
            P(None, "band", "member"),
            P(None, "band", "member"),
        ),
        out_specs=P("member", None, "band", None),
        check_vma=False,
    )
```

```python
import math

import jax
import jax.numpy as jnp
import numpy as np
from jax import lax
from jax.experimental import pallas as pl
from jax.experimental.pallas import tpu as pltpu
from jax.sharding import PartitionSpec as P

MESH = pl.DeviceIdType.MESH
BF16 = jnp.bfloat16
F32 = jnp.float32

phase_fraction = (0.625, 0.875, 0.125, 0.375)

KEN, LEVELS, NYC, NXC = 64, 16, 256, 512
BANDS, MEMBERS, XC, ZL = 16, 32, 8, 4
ZH, YB = 4, 4
BLOCK = NYC // ZH
LAT, LON = NYC // BANDS, NXC // MEMBERS
SCALE = 1.0 / math.sqrt(KEN - 1)


def cubic_weights(fraction):
    return (
        (-(fraction**3) + 2 * fraction**2 - fraction) / 2,
        (3 * fraction**3 - 5 * fraction**2 + 2) / 2,
        (-3 * fraction**3 + 4 * fraction**2 + fraction) / 2,
        (fraction**3 - fraction**2) / 2,
    )


def refine_rows(shift):
    w = np.zeros((64, 32), np.float32)
    for f in range(64):
        j, r = divmod(f + shift, 4)
        for tap, weight in enumerate(cubic_weights(phase_fraction[r])):
            w[f, j - 2 + tap + (r >= 2) + 8] += weight
    return w


def split_np(w):
    hi = w.astype(BF16)
    lo = (w - hi.astype(np.float32)).astype(BF16)
    return hi, lo


def constants():
    centre, ahead, behind = (refine_rows(s) for s in (0, 1, -1))
    lon = np.zeros((128, 12 * 128), np.float32)
    for s, w in enumerate((centre, ahead, behind)):
        for j in range(4):
            at = (4 * s + j) * 128
            lon[32 * j : 32 * j + 32, at : at + 64] = w.T
            lon[32 * j : 32 * j + 32, at + 64 : at + 128] = w.T
    lh, ll = split_np(lon)
    lon3 = np.concatenate([lh, lh, ll], axis=0)
    first = (np.arange(12 * 128) % 128 < 64)[:, None]
    th, tl = split_np(np.concatenate([lon.T * first, lon.T * ~first], axis=1))
    lont = np.stack([th, tl])
    lat = np.concatenate([centre, ahead, behind], axis=0)
    ah, al = split_np(lat)
    lat3 = np.concatenate([ah, al, ah], axis=1)
    bh, bl = split_np(np.ascontiguousarray(lat.T))
    latt3 = np.concatenate([bh, bl, bh], axis=1)
    ch, cl = split_np(np.ascontiguousarray(centre.T))
    lattc3 = np.concatenate([ch, cl, ch], axis=1)
    sel = np.zeros((512, 256), np.float32)
    for b in range(BANDS):
        for t in range(32):
            y = 16 * b - 8 + t
            if 0 <= y < NYC:
                sel[32 * b + t, y] = 1
    fold = np.zeros((32, 128), np.float32)
    for j in range(4):
        fold[np.arange(32), 32 * j + np.arange(32)] = 1
    return tuple(
        jnp.asarray(v, BF16)
        for v in (lon3, lont, lat3, latt3, lattc3, sel, np.ascontiguousarray(sel.T), fold)
    )


def split(x):
    hi = x.astype(BF16)
    return hi, (x - hi.astype(F32)).astype(BF16)


def dot(a, b):
    return jnp.dot(a, b, preferred_element_type=F32)


def dot_t(a, b):
    return lax.dot_general(a, b, (((1,), (1,)), ((), ())), preferred_element_type=F32)


def kernel(
    c_hbm, m_hbm, lon_hbm, lat_hbm, bal_hbm, inn_hbm, ow_hbm, *rest
):
    consts_hbm, (
        out,
        lonm, latm, bal_in, inn_in, ow_in,
        lon3, lont, lat3, latt3, lattc3, sel, selt, fold,
        gc, gm, ft, pt, pa, pbs, pb, pe, sw, z2, r2, ysc, c3, r3, ct, gq, ge, g4, cgt, gb, wsc, ob, cv,
        bh, bl, latf, ap3, atph, atpl, bal, inn, ow,
        send, recv, local, loads, ready,
    ) = rest[:8], rest[8:]
    me_m, me_b = lax.axis_index("member"), lax.axis_index("band")
    zl, xc = me_m // XC, me_m % XC
    zh, yb = me_b // YB, me_b % YB
    level = (me_b, lax.rem(me_b + BANDS - YB, BANDS))
    outer = (lax.rem(zh + ZH - 1, ZH), lax.rem(zh + 1, ZH))

    def band_peer(i):
        return lax.rem(me_b + 1 + lax.rem(i + 7, BANDS - 1), BANDS)

    def on_band(b):
        return {"member": me_m, "band": b}

    def on_member(m):
        return {"member": m, "band": me_b}

    def xc_peer(d):
        return zl * XC + lax.rem(xc + d, XC)

    def zl_peer(d):
        return lax.rem(zl + d, ZL) * XC + xc

    barrier = pltpu.get_barrier_semaphore()

    def greet(device):
        pl.semaphore_signal(barrier, inc=1, device_id=device, device_id_type=MESH)

    def ahead(y):
        return outer[1] * YB + lax.rem(yb + y, YB)

    def behind(y):
        return outer[0] * YB + lax.rem(yb + y, YB)

    def beside(y):
        return zh * YB + lax.rem(yb + y, YB)

    def to_east(z):
        return lax.rem(z * XC + xc + 1, MEMBERS)

    def to_west(z):
        return lax.rem(z * XC + xc + MEMBERS - 1, MEMBERS)

    @pl.loop(0, YB)
    def _(y):
        greet(on_band(ahead(y)))
        greet(on_band(behind(y)))

    @pl.loop(1, YB)
    def _(y):
        greet(on_band(beside(y)))

    @pl.loop(0, ZL)
    def _(z):
        greet(on_member(to_east(z)))
        greet(on_member(to_west(z)))

    @pl.loop(1, ZL)
    def _(d):
        greet(on_member(zl_peer(d)))

    @pl.loop(1, XC)
    def _(d):
        greet(on_member(xc_peer(d)))

    loaded = [
        pltpu.make_async_copy(src, dst, loads.at[n])
        for n, (src, dst) in enumerate(
            zip(
                (lon_hbm, lat_hbm, bal_hbm, inn_hbm, ow_hbm, *consts_hbm, c_hbm),
                (lonm, latm, bal_in, inn_in, ow_in, lon3, lont, lat3, latt3, lattc3, sel, selt, fold, cv),
            )
        )
    ]
    mine = pl.ds(pl.multiple_of(LAT * yb, LAT), LAT)
    mine_all = pl.ds(pl.multiple_of(LAT * me_b, LAT), LAT)
    own = [
        pltpu.make_async_copy(src.at[:, level[s]], dst.at[s, :, rows], local.at[s, n])
        for s in range(2)
        for n, (src, dst, rows) in enumerate(((c_hbm, gc, mine), (m_hbm, gm, mine_all)))
    ]
    for copy in loaded + own:
        copy.start()
    pl.semaphore_wait(barrier, 3 * YB - 1 + XC - 1 + ZL - 1 + 2 * ZL)
    pl.semaphore_signal(ready, inc=1, device_id=on_band(behind(0)), device_id_type=MESH)

    def push(src, dst, ph, device):
        pltpu.make_async_remote_copy(
            src_ref=src, dst_ref=dst, send_sem=send.at[ph], recv_sem=recv.at[ph],
            device_id=device, device_id_type=MESH,
        ).start()

    def wait_for(ref, sem):
        pltpu.make_async_copy(ref, ref, sem).wait()

    def level_at(b, slot):
        return b if slot == 0 else lax.rem(b + BANDS - YB, BANDS)

    def send_members(b, slot, ph):
        push(m_hbm.at[:, level_at(b, slot)], gm.at[slot, :, mine_all], ph, on_band(b))

    def send_controls(b, slot, half):
        rows = pl.ds(pl.multiple_of(BLOCK * half + LAT * yb, LAT), LAT)
        push(c_hbm.at[:, level_at(b, slot)], gc.at[slot, :, rows], slot, on_band(b))

    @pl.loop(0, YB)
    def _(y):
        send_members(ahead(y), 0, 2)
        send_members(behind(y), 1, 3)

    @pl.loop(0, YB)
    def _(y):
        send_controls(ahead(y), 0, 1)
        send_controls(behind(y), 1, 1)

    @pl.loop(1, YB)
    def _(y):
        send_controls(beside(y), 0, 0)
        send_controls(beside(y), 1, 0)

    @pl.loop(0, YB)
    def _(y):
        send_members(behind(y), 0, 4)
        send_members(ahead(y), 1, 5)

    @pl.loop(1, YB)
    def _(y):
        send_members(beside(y), 0, 4)
        send_members(beside(y), 1, 5)

    two = gm.at[0, 0, pl.ds(0, 8 * LAT)]
    seven = gm.at[0, 0, pl.ds(0, 14 * LAT)]

    def block(group):
        return pl.ds(pl.multiple_of(BLOCK * group, BLOCK), BLOCK)

    def relay():
        wait_for(two, recv.at[3])
        rows = block(outer[1])
        push(gm.at[1, :, rows], gm.at[0, :, rows], 6, on_band(outer[0] * YB + yb))
        wait_for(two, recv.at[2])
        rows = block(outer[0])
        push(gm.at[0, :, rows], gm.at[1, :, rows], 7, on_band(outer[1] * YB + yb))

    def prepare():
        for copy in loaded:
            copy.wait()
        for i in range(4):
            rows = pl.ds(128 * i, 128)
            bh[rows, :], bl[rows, :] = split(lonm[rows, :])
        for i in range(2):
            latf[:, pl.ds(128 * i, 128)] = latm[pl.ds(128 * i, 128), :].T
        for s in range(2):
            half = jnp.concatenate([latf[block(zh), :], latf[block(outer[s]), :]], axis=0)
            atph[s], atpl[s] = split(half)
            h, l = split(half.T)
            ap3[s] = jnp.concatenate([h, l, h], axis=1)
        for n in range(5):
            bal[n] = jnp.concatenate([bal_in[n], bal_in[n]], axis=1)
        for p in range(LEVELS // 2):
            inn[p] = jnp.concatenate([inn_in[2 * p], inn_in[2 * p + 1]], axis=1)
            ow[p] = jnp.concatenate([ow_in[2 * p], ow_in[2 * p + 1]], axis=1)
        row = lax.broadcasted_iota(jnp.int32, (64, 128), 0)
        bal[3] = jnp.where((row == 63) & (me_b == BANDS - 1), 0.0, bal[3])
        bal[4] = jnp.where((row == 0) & (me_b == 0), 0.0, bal[4])

    def fields():
        for copy in own:
            copy.wait()
        wait_for(seven, recv.at[0])
        wait_for(seven, recv.at[1])

        @pl.loop(0, 2)
        def _(s):
            @pl.loop(0, 2)
            def _(k):
                ch, cl = split(gc[s, k])
                x = dot_t(ch, bh[...]) + dot_t(cl, bh[...]) + dot_t(ch, bl[...])
                xh, xl = split(x)
                ft[s, k] = dot(ap3[s], jnp.concatenate([xh, xh, xl], axis=0))

    def products(s):
        wait_for(seven, recv.at[4 + s])
        wait_for(two, recv.at[6 + s])
        for i in range(ZL):
            at = pl.ds(128 * i, 128)
            p = (gm[s, 0, :, at] * ft[s, 0, :, at] + gm[s, 1, :, at] * ft[s, 1, :, at]) * SCALE
            pt[s, i] = p.T.reshape(XC, LON, NYC)

        @pl.loop(1, XC)
        def _(d):
            p = xc_peer(d)
            push(pt.at[s, :, lax.rem(p, XC)], pa.at[s, xc], 8 + s, on_member(p))

        pa[s, xc] = pt[s, :, xc]

    def reduce_b():
        for s in range(2):
            wait_for(pa.at[s, pl.ds(0, XC - 1)], recv.at[8 + s])
            total = pa[s, 0]
            for i in range(1, XC):
                total = total + pa[s, i]
            pbs[:, s] = total

        @pl.loop(0, ZL)
        def _(z):
            push(pbs.at[z, :, pl.ds(8, 8)], pe.at[0, zl], 11, on_member(to_east(z)))
            push(pbs.at[z, :, pl.ds(0, 8)], pe.at[1, zl], 12, on_member(to_west(z)))

        @pl.loop(1, ZL)
        def _(d):
            p = zl_peer(d)
            push(pbs.at[p // XC], pb.at[zl], 10, on_member(p))

        pb[zl] = pbs[zl]

    def hand_out():
        wait_for(pb.at[pl.ds(0, ZL - 1)], recv.at[10])
        wait_for(pe.at[0], recv.at[11])
        wait_for(pe.at[1], recv.at[12])
        sw[:, pl.ds(8, LON)] = pb[0] + pb[1] + pb[2] + pb[3]
        sw[:, pl.ds(0, 8)] = pe[0, 0] + pe[0, 1] + pe[0, 2] + pe[0, 3]
        sw[:, pl.ds(24, 8)] = pe[1, 0] + pe[1, 1] + pe[1, 2] + pe[1, 3]
        w, v = sw[0], sw[1]
        wh, wl = split(jnp.concatenate([w, w, w, w, v, v, v, v], axis=0))
        z = dot_t(sel[...], wh) + dot_t(sel[...], wl)
        group = lax.broadcasted_iota(jnp.int32, (BANDS, 8, 128), 2) // 32
        for s in range(2):
            zs = z[:, 128 * s : 128 * s + 128].reshape(BANDS, 4, 8, 128)
            packed = zs[:, 0]
            for j in range(1, 4):
                packed = jnp.where(group == j, zs[:, j], packed)
            z2[:, s] = packed
        pl.semaphore_wait(ready, 1)

        @pl.loop(0, BANDS - 1)
        def _(i):
            b = band_peer(i)
            push(z2.at[b], r2.at[me_b], 13, on_band(b))

        r2[me_b] = z2[me_b]

    def fine():
        wait_for(r2.at[pl.ds(0, BANDS - 1)], recv.at[13])
        x = jnp.concatenate(
            [
                r2[lev, 0] + r2[(lev + YB) % BANDS, 1]
                for first in range(2)
                for lev in range(first, LEVELS, 2)
            ],
            axis=0,
        )
        xh, xl = split(x)
        y = dot(jnp.concatenate([xh, xl, xh], axis=1), lon3[...])
        left = lax.broadcasted_iota(jnp.int32, (4 * LEVELS, 128), 1) < 64
        for s in range(3):
            for j in range(4):
                at = slice((4 * s + j) * 128, (4 * s + j + 1) * 128)
                pair = jnp.where(left, y[: 4 * LEVELS, at], y[4 * LEVELS :, at])
                for p in range(LEVELS // 2):
                    ysc[s, pl.ds(8 * j, 8), pl.ds(128 * p, 128)] = pair[8 * p : 8 * p + 8]

        def stacked(v):
            h, l = split(v)
            return jnp.concatenate([h, h, l], axis=0)

        v_c = dot(lat3[...], stacked(ysc[0]))
        v_e = dot(lat3[pl.ds(0, 64), :], stacked(ysc[1]))
        v_w = dot(lat3[pl.ds(0, 64), :], stacked(ysc[2]))
        to_c, to_e, to_w = [], [], []
        for p in range(LEVELS // 2):
            at = slice(128 * p, 128 * p + 128)
            image = (
                bal[0] * v_c[0:64, at] + bal[1] * v_e[:, at] + bal[2] * v_w[:, at]
                + bal[3] * v_c[64:128, at] + bal[4] * v_c[128:192, at]
            )
            misfit = ow[p] * (image - inn[p])
            to_c.append(
                jnp.concatenate([bal[0] * misfit, bal[3] * misfit, bal[4] * misfit], axis=0)
            )
            to_e.append(bal[1] * misfit)
            to_w.append(bal[2] * misfit)
        t = (
            dot(latt3[...], stacked(jnp.concatenate(to_c, axis=1))),
            dot(lattc3[...], stacked(jnp.concatenate(to_e, axis=1))),
            dot(lattc3[...], stacked(jnp.concatenate(to_w, axis=1))),
        )
        rows = []
        for p in range(LEVELS // 2):
            rows.append(
                jnp.concatenate(
                    [
                        t[s][8 * j : 8 * j + 8, 128 * p : 128 * p + 128]
                        for s in range(3)
                        for j in range(4)
                    ],
                    axis=1,
                )
            )
        lh, ll = split(jnp.concatenate(rows, axis=0))
        c = dot(lh, lont[0]) + dot(ll, lont[0]) + dot(lh, lont[1])
        for lev in range(LEVELS):
            p, at = lev // 2, slice(128 * (lev % 2), 128 * (lev % 2) + 128)
            c3[lev, 0] = c[8 * p : 8 * p + 8, at]
            c3[(lev + YB) % BANDS, 1] = c[8 * p : 8 * p + 8, at]

        @pl.loop(0, BANDS - 1)
        def _(i):
            b = band_peer(i)
            push(c3.at[b], r3.at[me_b], 14, on_band(b))

        r3[me_b] = c3[me_b]

    def gather_in():
        wait_for(r3.at[pl.ds(0, BANDS - 1)], recv.at[14])
        group = lax.broadcasted_iota(jnp.int32, (BANDS, 8, 128), 2) // 32
        both = []
        for s in range(2):
            r = r3[:, s]
            e = jnp.stack([jnp.where(group == j, r, 0.0) for j in range(4)], axis=1)
            both.append(e.reshape(512, 128))
        eh, el = split(jnp.concatenate(both, axis=1))
        oh, ol = split(dot(selt[...], eh) + dot(selt[...], el))
        for s in range(2):
            at = slice(128 * s, 128 * s + 128)
            ct[s] = dot_t(fold[...], oh[:, at]) + dot_t(fold[...], ol[:, at])
        tile_w = lax.rem(me_m + MEMBERS - 1, MEMBERS) // XC
        tile_e = lax.rem(me_m + 1, MEMBERS) // XC

        @pl.loop(0, ZL)
        def _(z):
            push(ct.at[:, pl.ds(0, 8)], ge.at[1, tile_w], 15, on_member(to_west(z)))
            push(ct.at[:, pl.ds(24, 8)], ge.at[0, tile_e], 16, on_member(to_east(z)))

        @pl.loop(1, ZL)
        def _(d):
            push(ct.at[:, pl.ds(8, LON)], gq.at[zl], 17, on_member(zl_peer(d)))

        gq[zl] = ct[:, pl.ds(8, LON)]

    def spread_a():
        wait_for(gq.at[pl.ds(0, ZL - 1)], recv.at[17])
        wait_for(ge.at[1], recv.at[15])
        wait_for(ge.at[0], recv.at[16])
        for s in range(2):
            for z in range(ZL):
                g4[s, z, pl.ds(0, 8)] = (gq[z, s, pl.ds(0, 8)] + ge[0, z, s]) * SCALE
                g4[s, z, pl.ds(8, 8)] = (gq[z, s, pl.ds(8, 8)] + ge[1, z, s]) * SCALE

            @pl.loop(1, XC)
            def _(d):
                push(g4.at[s], cgt.at[s, :, xc], 18 + s, on_member(xc_peer(d)))

            cgt[s, :, xc] = g4[s]

    def weigh(s):
        wait_for(cgt.at[s, :, pl.ds(0, XC - 1)], recv.at[18 + s])
        for i in range(ZL):
            at = pl.ds(128 * i, 128)
            g = cgt[s, i].reshape(128, NYC).T
            for k in range(2):
                w = gm[s, k, :, at] * g
                h = w.astype(BF16)
                wsc[s, 0, k, :, at] = h
                wsc[s, 1, k, :, at] = (w - h.astype(F32)).astype(BF16)

    def adjoint(s, half):
        rows = pl.ds(BLOCK * half, BLOCK)
        ph, plo = atph[s, rows], atpl[s, rows]
        t = jnp.concatenate(
            [
                dot(ph, wsc[s, 0, k]) + dot(plo, wsc[s, 0, k]) + dot(ph, wsc[s, 1, k])
                for k in range(2)
            ],
            axis=0,
        )
        th, tl = split(t)
        g = dot(th, bh[...]) + dot(tl, bh[...]) + dot(th, bl[...])
        gb[s, 0, rows] = g[:BLOCK]
        gb[s, 1, rows] = g[BLOCK:]
        to = (behind, ahead)[s] if half else beside

        @pl.loop(0 if half else 1, YB)
        def _(y):
            rows = pl.ds(pl.multiple_of(BLOCK * half + LAT * lax.rem(yb + y, YB), LAT), LAT)
            push(gb.at[s, :, rows], ob.at[:, level[s]], 20 + s, on_band(to(y)))

        if not half:
            ob[:, level[s]] = gb[s, :, mine, :]

    def finish():
        for s in range(2):
            wait_for(seven, recv.at[20 + s])
        out[...] = ob[...] + cv[...]
        for ph in (0, 1, 4, 5, 20, 21):
            wait_for(seven, send.at[ph])
        for ph in (2, 3, 6, 7):
            wait_for(two, send.at[ph])
        for s in range(2):
            wait_for(pa.at[s, pl.ds(0, XC - 1)], send.at[8 + s])
            wait_for(pa.at[s, pl.ds(0, XC - 1)], send.at[18 + s])
        wait_for(pb.at[pl.ds(0, ZL - 1)], send.at[10])
        wait_for(pb.at[pl.ds(0, ZL - 1)], send.at[17])
        for ph in (11, 12, 15, 16):
            wait_for(pe.at[0], send.at[ph])
        wait_for(r2.at[pl.ds(0, BANDS - 1)], send.at[13])
        wait_for(r3.at[pl.ds(0, BANDS - 1)], send.at[14])

    relay()
    prepare()
    fields()
    products(0)
    products(1)
    reduce_b()
    hand_out()
    fine()
    gather_in()
    spread_a()
    weigh(0)
    adjoint(0, 1)
    weigh(1)
    adjoint(1, 1)
    adjoint(0, 0)
    adjoint(1, 0)
    finish()


def body(controls, members, loc_lon, loc_lat, balance, innovation, obs_weight):
    consts = constants()
    hbm = pl.BlockSpec(memory_space=pl.ANY)
    vmem = pl.BlockSpec(memory_space=pltpu.VMEM)
    f32 = lambda *s: pltpu.VMEM(s, F32)
    b16 = lambda *s: pltpu.VMEM(s, BF16)
    small = (loc_lon, loc_lat, balance, innovation, obs_weight)
    return pl.pallas_call(
        kernel,
        out_shape=jax.ShapeDtypeStruct(controls.shape, F32),
        in_specs=[hbm] * (7 + len(consts)),
        out_specs=vmem,
        scratch_shapes=[pltpu.VMEM(v.shape, v.dtype) for v in (*small, *consts)]
        + [
            f32(2, 2, 2 * BLOCK, NXC),
            f32(2, 2, NYC, NXC),
            f32(2, 2, NYC, NXC),
            f32(2, ZL, XC, LON, NYC),
            f32(2, XC, ZL, LON, NYC),
            f32(ZL, 2, LON, NYC),
            f32(ZL, 2, LON, NYC),
            f32(2, ZL, 2, 8, NYC),
            f32(2, 32, NYC),
            f32(BANDS, 2, 8, 128),
            f32(BANDS, 2, 8, 128),
            f32(3, 32, LEVELS * 64),
            f32(BANDS, 2, 8, 128),
            f32(BANDS, 2, 8, 128),
            f32(2, 32, NYC),
            f32(ZL, 2, LON, NYC),
            f32(2, ZL, 2, 8, NYC),
            f32(2, ZL, LON, NYC),
            f32(2, ZL, XC, LON, NYC),
            f32(2, 2, 2 * BLOCK, NXC),
            b16(2, 2, 2, NYC, NXC),
            pltpu.VMEM(controls.shape, F32),
            pltpu.VMEM(controls.shape, F32),
            b16(NXC, NXC), b16(NXC, NXC), f32(NYC, NYC),
            b16(2, NYC, 6 * BLOCK), b16(2, 2 * BLOCK, NYC), b16(2, 2 * BLOCK, NYC),
            f32(5, 64, 128), f32(LEVELS // 2, 64, 128), f32(LEVELS // 2, 64, 128),
            pltpu.SemaphoreType.DMA((22,)),
            pltpu.SemaphoreType.DMA((22,)),
            pltpu.SemaphoreType.DMA((2, 2)),
            pltpu.SemaphoreType.DMA((14,)),
            pltpu.SemaphoreType.REGULAR,
        ],
        compiler_params=pltpu.CompilerParams(
            collective_id=0, has_side_effects=True, vmem_limit_bytes=56 << 20
        ),
        name="gradient",
    )(controls, members, *small, *consts)


def solution(mesh):
    return jax.shard_map(
        body,
        mesh=mesh,
        in_specs=(
            P("member", None, "band", None),
            P("member", None, "band", None),
            P(),
            P(),
            P(None, "band", "member"),
            P(None, "band", "member"),
            P(None, "band", "member"),
        ),
        out_specs=P("member", None, "band", None),
        check_vma=False,
    )
```

```python
import math

import jax
import jax.numpy as jnp
import numpy as np
from jax import lax
from jax.experimental import pallas as pl
from jax.experimental.pallas import tpu as pltpu
from jax.sharding import PartitionSpec as P

MESH = pl.DeviceIdType.MESH
BF16 = jnp.bfloat16
F32 = jnp.float32

phase_fraction = (0.625, 0.875, 0.125, 0.375)

KEN, LEVELS, NYC, NXC = 64, 16, 256, 512
BANDS, MEMBERS, XC, ZL = 16, 32, 8, 4
ZH, YB = 4, 4
BLOCK = NYC // ZH
LAT, LON = NYC // BANDS, NXC // MEMBERS
SCALE = 1.0 / math.sqrt(KEN - 1)


def cubic_weights(fraction):
    return (
        (-(fraction**3) + 2 * fraction**2 - fraction) / 2,
        (3 * fraction**3 - 5 * fraction**2 + 2) / 2,
        (-3 * fraction**3 + 4 * fraction**2 + fraction) / 2,
        (fraction**3 - fraction**2) / 2,
    )


def refine_rows(shift):
    w = np.zeros((64, 32), np.float32)
    for f in range(64):
        j, r = divmod(f + shift, 4)
        for tap, weight in enumerate(cubic_weights(phase_fraction[r])):
            w[f, j - 2 + tap + (r >= 2) + 8] += weight
    return w


def split_np(w):
    hi = w.astype(BF16)
    lo = (w - hi.astype(np.float32)).astype(BF16)
    return hi, lo


def constants():
    centre, ahead, behind = (refine_rows(s) for s in (0, 1, -1))
    lon = np.zeros((128, 12 * 128), np.float32)
    for s, w in enumerate((centre, ahead, behind)):
        for j in range(4):
            at = (4 * s + j) * 128
            lon[32 * j : 32 * j + 32, at : at + 64] = w.T
            lon[32 * j : 32 * j + 32, at + 64 : at + 128] = w.T
    lh, ll = split_np(lon)
    lon3 = np.concatenate([lh, lh, ll], axis=0)
    first = (np.arange(12 * 128) % 128 < 64)[:, None]
    th, tl = split_np(np.concatenate([lon.T * first, lon.T * ~first], axis=1))
    lont = np.stack([th, tl])
    lat = np.concatenate([centre, ahead, behind], axis=0)
    ah, al = split_np(lat)
    lat3 = np.concatenate([ah, al, ah], axis=1)
    bh, bl = split_np(np.ascontiguousarray(lat.T))
    latt3 = np.concatenate([bh, bl, bh], axis=1)
    ch, cl = split_np(np.ascontiguousarray(centre.T))
    lattc3 = np.concatenate([ch, cl, ch], axis=1)
    sel = np.zeros((512, 256), np.float32)
    for b in range(BANDS):
        for t in range(32):
            y = 16 * b - 8 + t
            if 0 <= y < NYC:
                sel[32 * b + t, y] = 1
    fold = np.zeros((32, 128), np.float32)
    for j in range(4):
        fold[np.arange(32), 32 * j + np.arange(32)] = 1
    return tuple(
        jnp.asarray(v, BF16)
        for v in (lon3, lont, lat3, latt3, lattc3, sel, np.ascontiguousarray(sel.T), fold)
    )


def split(x):
    hi = x.astype(BF16)
    return hi, (x - hi.astype(F32)).astype(BF16)


def dot(a, b):
    return jnp.dot(a, b, preferred_element_type=F32)


def dot_t(a, b):
    return lax.dot_general(a, b, (((1,), (1,)), ((), ())), preferred_element_type=F32)


def kernel(
    c_hbm, m_hbm, lon_hbm, lat_hbm, bal_hbm, inn_hbm, ow_hbm, *rest
):
    consts_hbm, (
        out,
        lonm, latm, bal_in, inn_in, ow_in,
        lon3, lont, lat3, latt3, lattc3, sel, selt, fold,
        gc, gm, ft, pt, pc, ps, pa, pbs, pb, sw, z2, r2, ysc, c3, r3, ct, hl, g4, cgt, gb, wsc, ob, cv,
        bh, bl, latf, ap3, atph, atpl, bal, inn, ow,
        send, recv, local, loads, ready,
    ) = rest[:8], rest[8:]
    me_m, me_b = lax.axis_index("member"), lax.axis_index("band")
    zl, xc = me_m // XC, me_m % XC
    xx, core = xc // 2, xc % 2
    zh, yb = me_b // YB, me_b % YB
    level = (me_b, lax.rem(me_b + BANDS - YB, BANDS))
    outer = (lax.rem(zh + ZH - 1, ZH), lax.rem(zh + 1, ZH))

    def band_peer(i):
        return lax.rem(me_b + 1 + lax.rem(i + 7, BANDS - 1), BANDS)

    def on_band(b):
        return {"member": me_m, "band": b}

    def on_member(m):
        return {"member": m, "band": me_b}

    def x_peer(d):
        return zl * XC + lax.rem(xx + d, XC // 2) * 2 + core

    other = zl * XC + 2 * xx + 1 - core
    east, west = lax.rem(me_m + 1, MEMBERS), lax.rem(me_m + MEMBERS - 1, MEMBERS)

    def zl_peer(d):
        return lax.rem(zl + d, ZL) * XC + xc

    barrier = pltpu.get_barrier_semaphore()

    def greet(device):
        pl.semaphore_signal(barrier, inc=1, device_id=device, device_id_type=MESH)

    def ahead(y):
        return outer[1] * YB + lax.rem(yb + y, YB)

    def behind(y):
        return outer[0] * YB + lax.rem(yb + y, YB)

    def beside(y):
        return zh * YB + lax.rem(yb + y, YB)

    @pl.loop(0, YB)
    def _(y):
        greet(on_band(ahead(y)))
        greet(on_band(behind(y)))

    @pl.loop(1, YB)
    def _(y):
        greet(on_band(beside(y)))

    greet(on_member(east))
    greet(on_member(west))
    greet(on_member(other))

    @pl.loop(1, ZL)
    def _(d):
        greet(on_member(zl_peer(d)))

    @pl.loop(1, XC // 2)
    def _(d):
        greet(on_member(x_peer(d)))

    loaded = [
        pltpu.make_async_copy(src, dst, loads.at[n])
        for n, (src, dst) in enumerate(
            zip(
                (lon_hbm, lat_hbm, bal_hbm, inn_hbm, ow_hbm, *consts_hbm, c_hbm),
                (lonm, latm, bal_in, inn_in, ow_in, lon3, lont, lat3, latt3, lattc3, sel, selt, fold, cv),
            )
        )
    ]
    mine = pl.ds(pl.multiple_of(LAT * yb, LAT), LAT)
    mine_all = pl.ds(pl.multiple_of(LAT * me_b, LAT), LAT)
    own = [
        pltpu.make_async_copy(src.at[:, level[s]], dst.at[s, :, rows], local.at[s, n])
        for s in range(2)
        for n, (src, dst, rows) in enumerate(((c_hbm, gc, mine), (m_hbm, gm, mine_all)))
    ]
    for copy in loaded + own:
        copy.start()
    pl.semaphore_wait(barrier, 3 * YB - 1 + XC // 2 - 1 + ZL - 1 + 3)
    pl.semaphore_signal(ready, inc=1, device_id=on_band(behind(0)), device_id_type=MESH)

    def push(src, dst, ph, device):
        pltpu.make_async_remote_copy(
            src_ref=src, dst_ref=dst, send_sem=send.at[ph], recv_sem=recv.at[ph],
            device_id=device, device_id_type=MESH,
        ).start()

    def wait_for(ref, sem):
        pltpu.make_async_copy(ref, ref, sem).wait()

    def level_at(b, slot):
        return b if slot == 0 else lax.rem(b + BANDS - YB, BANDS)

    def send_members(b, slot, ph):
        push(m_hbm.at[:, level_at(b, slot)], gm.at[slot, :, mine_all], ph, on_band(b))

    def send_controls(b, slot, half):
        rows = pl.ds(pl.multiple_of(BLOCK * half + LAT * yb, LAT), LAT)
        push(c_hbm.at[:, level_at(b, slot)], gc.at[slot, :, rows], slot, on_band(b))

    @pl.loop(0, YB)
    def _(y):
        send_members(ahead(y), 0, 2)
        send_members(behind(y), 1, 3)

    @pl.loop(0, YB)
    def _(y):
        send_controls(ahead(y), 0, 1)
        send_controls(behind(y), 1, 1)

    @pl.loop(1, YB)
    def _(y):
        send_controls(beside(y), 0, 0)
        send_controls(beside(y), 1, 0)

    @pl.loop(0, YB)
    def _(y):
        send_members(behind(y), 0, 4)
        send_members(ahead(y), 1, 5)

    @pl.loop(1, YB)
    def _(y):
        send_members(beside(y), 0, 4)
        send_members(beside(y), 1, 5)

    two = gm.at[0, 0, pl.ds(0, 8 * LAT)]
    seven = gm.at[0, 0, pl.ds(0, 14 * LAT)]

    def block(group):
        return pl.ds(pl.multiple_of(BLOCK * group, BLOCK), BLOCK)

    def relay():
        wait_for(two, recv.at[3])
        rows = block(outer[1])
        push(gm.at[1, :, rows], gm.at[0, :, rows], 6, on_band(outer[0] * YB + yb))
        wait_for(two, recv.at[2])
        rows = block(outer[0])
        push(gm.at[0, :, rows], gm.at[1, :, rows], 7, on_band(outer[1] * YB + yb))

    def prepare():
        for copy in loaded:
            copy.wait()
        for i in range(4):
            rows = pl.ds(128 * i, 128)
            bh[rows, :], bl[rows, :] = split(lonm[rows, :])
        for i in range(2):
            latf[:, pl.ds(128 * i, 128)] = latm[pl.ds(128 * i, 128), :].T
        for s in range(2):
            half = jnp.concatenate([latf[block(zh), :], latf[block(outer[s]), :]], axis=0)
            atph[s], atpl[s] = split(half)
            h, l = split(half.T)
            ap3[s] = jnp.concatenate([h, l, h], axis=1)
        for n in range(5):
            bal[n] = jnp.concatenate([bal_in[n], bal_in[n]], axis=1)
        for p in range(LEVELS // 2):
            inn[p] = jnp.concatenate([inn_in[2 * p], inn_in[2 * p + 1]], axis=1)
            ow[p] = jnp.concatenate([ow_in[2 * p], ow_in[2 * p + 1]], axis=1)
        row = lax.broadcasted_iota(jnp.int32, (64, 128), 0)
        bal[3] = jnp.where((row == 63) & (me_b == BANDS - 1), 0.0, bal[3])
        bal[4] = jnp.where((row == 0) & (me_b == 0), 0.0, bal[4])

    def fields():
        for copy in own:
            copy.wait()
        wait_for(seven, recv.at[0])
        wait_for(seven, recv.at[1])

        @pl.loop(0, 2)
        def _(s):
            @pl.loop(0, 2)
            def _(k):
                ch, cl = split(gc[s, k])
                x = dot_t(ch, bh[...]) + dot_t(cl, bh[...]) + dot_t(ch, bl[...])
                xh, xl = split(x)
                ft[s, k] = dot(ap3[s], jnp.concatenate([xh, xh, xl], axis=0))

    def products(s):
        wait_for(seven, recv.at[4 + s])
        wait_for(two, recv.at[6 + s])
        for i in range(ZL):
            at = pl.ds(128 * i, 128)
            p = (gm[s, 0, :, at] * ft[s, 0, :, at] + gm[s, 1, :, at] * ft[s, 1, :, at]) * SCALE
            pt[s, i] = p.T.reshape(XC // 2, 2, LON, NYC)

        push(pt.at[s, :, :, 1 - core], pc.at[s], 22 + s, on_member(other))

    def reduce_a(s):
        wait_for(pc.at[s], recv.at[22 + s])
        for z in range(ZL):
            ps[s, :, z] = pt[s, z, :, core] + pc[s, z]

        @pl.loop(1, XC // 2)
        def _(d):
            p = lax.rem(xx + d, XC // 2)
            push(ps.at[s, p], pa.at[s, xx], 8 + s, on_member(x_peer(d)))

        pa[s, xx] = ps[s, xx]

    def reduce_b():
        for s in range(2):
            wait_for(pa.at[s, pl.ds(0, XC // 2 - 1)], recv.at[8 + s])
            pbs[:, s] = pa[s, 0] + pa[s, 1] + pa[s, 2] + pa[s, 3]

        @pl.loop(1, ZL)
        def _(d):
            p = zl_peer(d)
            push(pbs.at[p // XC], pb.at[zl], 10, on_member(p))

        pb[zl] = pbs[zl]

    def halo():
        wait_for(pb.at[pl.ds(0, ZL - 1)], recv.at[10])
        sw[:, pl.ds(8, LON)] = pb[0] + pb[1] + pb[2] + pb[3]
        push(sw.at[:, pl.ds(8, 8)], sw.at[:, pl.ds(24, 8)], 11, on_member(west))
        push(sw.at[:, pl.ds(16, 8)], sw.at[:, pl.ds(0, 8)], 12, on_member(east))

    def hand_out():
        wait_for(sw.at[:, pl.ds(24, 8)], recv.at[11])
        wait_for(sw.at[:, pl.ds(0, 8)], recv.at[12])
        w, v = sw[0], sw[1]
        wh, wl = split(jnp.concatenate([w, w, w, w, v, v, v, v], axis=0))
        z = dot_t(sel[...], wh) + dot_t(sel[...], wl)
        group = lax.broadcasted_iota(jnp.int32, (BANDS, 8, 128), 2) // 32
        for s in range(2):
            zs = z[:, 128 * s : 128 * s + 128].reshape(BANDS, 4, 8, 128)
            packed = zs[:, 0]
            for j in range(1, 4):
                packed = jnp.where(group == j, zs[:, j], packed)
            z2[:, s] = packed
        pl.semaphore_wait(ready, 1)

        @pl.loop(0, BANDS - 1)
        def _(i):
            b = band_peer(i)
            push(z2.at[b], r2.at[me_b], 13, on_band(b))

        r2[me_b] = z2[me_b]

    def fine():
        wait_for(r2.at[pl.ds(0, BANDS - 1)], recv.at[13])
        x = jnp.concatenate(
            [
                r2[lev, 0] + r2[(lev + YB) % BANDS, 1]
                for first in range(2)
                for lev in range(first, LEVELS, 2)
            ],
            axis=0,
        )
        xh, xl = split(x)
        y = dot(jnp.concatenate([xh, xl, xh], axis=1), lon3[...])
        left = lax.broadcasted_iota(jnp.int32, (4 * LEVELS, 128), 1) < 64
        for s in range(3):
            for j in range(4):
                at = slice((4 * s + j) * 128, (4 * s + j + 1) * 128)
                pair = jnp.where(left, y[: 4 * LEVELS, at], y[4 * LEVELS :, at])
                for p in range(LEVELS // 2):
                    ysc[s, pl.ds(8 * j, 8), pl.ds(128 * p, 128)] = pair[8 * p : 8 * p + 8]

        def stacked(v):
            h, l = split(v)
            return jnp.concatenate([h, h, l], axis=0)

        v_c = dot(lat3[...], stacked(ysc[0]))
        v_e = dot(lat3[pl.ds(0, 64), :], stacked(ysc[1]))
        v_w = dot(lat3[pl.ds(0, 64), :], stacked(ysc[2]))
        to_c, to_e, to_w = [], [], []
        for p in range(LEVELS // 2):
            at = slice(128 * p, 128 * p + 128)
            image = (
                bal[0] * v_c[0:64, at] + bal[1] * v_e[:, at] + bal[2] * v_w[:, at]
                + bal[3] * v_c[64:128, at] + bal[4] * v_c[128:192, at]
            )
            misfit = ow[p] * (image - inn[p])
            to_c.append(
                jnp.concatenate([bal[0] * misfit, bal[3] * misfit, bal[4] * misfit], axis=0)
            )
            to_e.append(bal[1] * misfit)
            to_w.append(bal[2] * misfit)
        t = (
            dot(latt3[...], stacked(jnp.concatenate(to_c, axis=1))),
            dot(lattc3[...], stacked(jnp.concatenate(to_e, axis=1))),
            dot(lattc3[...], stacked(jnp.concatenate(to_w, axis=1))),
        )
        rows = []
        for p in range(LEVELS // 2):
            rows.append(
                jnp.concatenate(
                    [
                        t[s][8 * j : 8 * j + 8, 128 * p : 128 * p + 128]
                        for s in range(3)
                        for j in range(4)
                    ],
                    axis=1,
                )
            )
        lh, ll = split(jnp.concatenate(rows, axis=0))
        c = dot(lh, lont[0]) + dot(ll, lont[0]) + dot(lh, lont[1])
        for lev in range(LEVELS):
            p, at = lev // 2, slice(128 * (lev % 2), 128 * (lev % 2) + 128)
            c3[lev, 0] = c[8 * p : 8 * p + 8, at]
            c3[(lev + YB) % BANDS, 1] = c[8 * p : 8 * p + 8, at]

        @pl.loop(0, BANDS - 1)
        def _(i):
            b = band_peer(i)
            push(c3.at[b], r3.at[me_b], 14, on_band(b))

        r3[me_b] = c3[me_b]

    def gather_in():
        wait_for(r3.at[pl.ds(0, BANDS - 1)], recv.at[14])
        group = lax.broadcasted_iota(jnp.int32, (BANDS, 8, 128), 2) // 32
        both = []
        for s in range(2):
            r = r3[:, s]
            e = jnp.stack([jnp.where(group == j, r, 0.0) for j in range(4)], axis=1)
            both.append(e.reshape(512, 128))
        eh, el = split(jnp.concatenate(both, axis=1))
        oh, ol = split(dot(selt[...], eh) + dot(selt[...], el))
        for s in range(2):
            at = slice(128 * s, 128 * s + 128)
            ct[s] = dot_t(fold[...], oh[:, at]) + dot_t(fold[...], ol[:, at])
        push(ct.at[:, pl.ds(0, 8)], hl.at[1], 15, on_member(west))
        push(ct.at[:, pl.ds(24, 8)], hl.at[0], 16, on_member(east))

    def spread_b():
        wait_for(hl.at[1], recv.at[15])
        wait_for(hl.at[0], recv.at[16])
        own_part = ct[:, pl.ds(8, LON)] + jnp.concatenate([hl[0], hl[1]], axis=1)
        g4[zl] = own_part * SCALE

        @pl.loop(1, ZL)
        def _(d):
            push(g4.at[zl], g4.at[zl], 17, on_member(zl_peer(d)))

    def spread_a():
        wait_for(g4.at[pl.ds(0, ZL - 1)], recv.at[17])
        for s in range(2):

            @pl.loop(1, XC // 2)
            def _(d):
                push(g4.at[:, s], cgt.at[s, core, xx], 18 + s, on_member(x_peer(d)))

            cgt[s, core, xx] = g4[:, s]

    def spread_core(s):
        wait_for(cgt.at[s, 0, pl.ds(0, XC // 2 - 1)], recv.at[18 + s])
        push(cgt.at[s, core], cgt.at[s, core], 24 + s, on_member(other))

    def weigh(s):
        wait_for(cgt.at[s, 0], recv.at[24 + s])
        for i in range(ZL):
            at = pl.ds(128 * i, 128)
            g = jnp.concatenate(
                [cgt[s, c, x, i] for x in range(XC // 2) for c in range(2)], axis=0
            ).T
            for k in range(2):
                w = gm[s, k, :, at] * g
                h = w.astype(BF16)
                wsc[s, 0, k, :, at] = h
                wsc[s, 1, k, :, at] = (w - h.astype(F32)).astype(BF16)

    def adjoint(s, half):
        rows = pl.ds(BLOCK * half, BLOCK)
        ph, plo = atph[s, rows], atpl[s, rows]
        t = jnp.concatenate(
            [
                dot(ph, wsc[s, 0, k]) + dot(plo, wsc[s, 0, k]) + dot(ph, wsc[s, 1, k])
                for k in range(2)
            ],
            axis=0,
        )
        th, tl = split(t)
        g = dot(th, bh[...]) + dot(tl, bh[...]) + dot(th, bl[...])
        gb[s, 0, rows] = g[:BLOCK]
        gb[s, 1, rows] = g[BLOCK:]
        to = (behind, ahead)[s] if half else beside

        @pl.loop(0 if half else 1, YB)
        def _(y):
            rows = pl.ds(pl.multiple_of(BLOCK * half + LAT * lax.rem(yb + y, YB), LAT), LAT)
            push(gb.at[s, :, rows], ob.at[:, level[s]], 20 + s, on_band(to(y)))

        if not half:
            ob[:, level[s]] = gb[s, :, mine, :]

    def finish():
        for s in range(2):
            wait_for(seven, recv.at[20 + s])
        out[...] = ob[...] + cv[...]
        for ph in (0, 1, 4, 5, 20, 21):
            wait_for(seven, send.at[ph])
        for ph in (2, 3, 6, 7):
            wait_for(two, send.at[ph])
        for s in range(2):
            wait_for(pc.at[s], send.at[22 + s])
            wait_for(pc.at[s], send.at[24 + s])
            wait_for(pa.at[s, pl.ds(0, XC // 2 - 1)], send.at[8 + s])
            wait_for(pa.at[s, pl.ds(0, XC // 2 - 1)], send.at[18 + s])
        wait_for(pb.at[pl.ds(0, ZL - 1)], send.at[10])
        wait_for(pb.at[pl.ds(0, ZL - 1)], send.at[17])
        for ph in (11, 12, 15, 16):
            wait_for(hl.at[0], send.at[ph])
        wait_for(r2.at[pl.ds(0, BANDS - 1)], send.at[13])
        wait_for(r3.at[pl.ds(0, BANDS - 1)], send.at[14])

    relay()
    prepare()
    fields()
    products(0)
    products(1)
    reduce_a(0)
    reduce_a(1)
    reduce_b()
    halo()
    hand_out()
    fine()
    gather_in()
    spread_b()
    spread_a()
    spread_core(0)
    spread_core(1)
    weigh(0)
    adjoint(0, 1)
    weigh(1)
    adjoint(1, 1)
    adjoint(0, 0)
    adjoint(1, 0)
    finish()


def body(controls, members, loc_lon, loc_lat, balance, innovation, obs_weight):
    consts = constants()
    hbm = pl.BlockSpec(memory_space=pl.ANY)
    vmem = pl.BlockSpec(memory_space=pltpu.VMEM)
    f32 = lambda *s: pltpu.VMEM(s, F32)
    b16 = lambda *s: pltpu.VMEM(s, BF16)
    small = (loc_lon, loc_lat, balance, innovation, obs_weight)
    return pl.pallas_call(
        kernel,
        out_shape=jax.ShapeDtypeStruct(controls.shape, F32),
        in_specs=[hbm] * (7 + len(consts)),
        out_specs=vmem,
        scratch_shapes=[pltpu.VMEM(v.shape, v.dtype) for v in (*small, *consts)]
        + [
            f32(2, 2, 2 * BLOCK, NXC),
            f32(2, 2, NYC, NXC),
            f32(2, 2, NYC, NXC),
            f32(2, ZL, XC // 2, 2, LON, NYC),
            f32(2, ZL, XC // 2, LON, NYC),
            f32(2, XC // 2, ZL, LON, NYC),
            f32(2, XC // 2, ZL, LON, NYC),
            f32(ZL, 2, LON, NYC),
            f32(ZL, 2, LON, NYC),
            f32(2, 32, NYC),
            f32(BANDS, 2, 8, 128),
            f32(BANDS, 2, 8, 128),
            f32(3, 32, LEVELS * 64),
            f32(BANDS, 2, 8, 128),
            f32(BANDS, 2, 8, 128),
            f32(2, 32, NYC),
            f32(2, 2, 8, NYC),
            f32(ZL, 2, LON, NYC),
            f32(2, 2, XC // 2, ZL, LON, NYC),
            f32(2, 2, 2 * BLOCK, NXC),
            b16(2, 2, 2, NYC, NXC),
            pltpu.VMEM(controls.shape, F32),
            pltpu.VMEM(controls.shape, F32),
            b16(NXC, NXC), b16(NXC, NXC), f32(NYC, NYC),
            b16(2, NYC, 6 * BLOCK), b16(2, 2 * BLOCK, NYC), b16(2, 2 * BLOCK, NYC),
            f32(5, 64, 128), f32(LEVELS // 2, 64, 128), f32(LEVELS // 2, 64, 128),
            pltpu.SemaphoreType.DMA((26,)),
            pltpu.SemaphoreType.DMA((26,)),
            pltpu.SemaphoreType.DMA((2, 2)),
            pltpu.SemaphoreType.DMA((14,)),
            pltpu.SemaphoreType.REGULAR,
        ],
        compiler_params=pltpu.CompilerParams(
            collective_id=0, has_side_effects=True, vmem_limit_bytes=56 << 20
        ),
        name="gradient",
    )(controls, members, *small, *consts)


def solution(mesh):
    return jax.shard_map(
        body,
        mesh=mesh,
        in_specs=(
            P("member", None, "band", None),
            P("member", None, "band", None),
            P(),
            P(),
            P(None, "band", "member"),
            P(None, "band", "member"),
            P(None, "band", "member"),
        ),
        out_specs=P("member", None, "band", None),
        check_vma=False,
    )
```

```python
import math

import jax
import jax.numpy as jnp
import numpy as np
from jax import lax
from jax.experimental import pallas as pl
from jax.experimental.pallas import tpu as pltpu
from jax.sharding import PartitionSpec as P

MESH = pl.DeviceIdType.MESH
BF16 = jnp.bfloat16
F32 = jnp.float32

phase_fraction = (0.625, 0.875, 0.125, 0.375)

KEN, LEVELS, NYC, NXC = 64, 16, 256, 512
BANDS, MEMBERS, XC, ZL = 16, 32, 8, 4
ZH, YB = 4, 4
BLOCK = NYC // ZH
LAT, LON = NYC // BANDS, NXC // MEMBERS
SCALE = 1.0 / math.sqrt(KEN - 1)


def cubic_weights(fraction):
    return (
        (-(fraction**3) + 2 * fraction**2 - fraction) / 2,
        (3 * fraction**3 - 5 * fraction**2 + 2) / 2,
        (-3 * fraction**3 + 4 * fraction**2 + fraction) / 2,
        (fraction**3 - fraction**2) / 2,
    )


def refine_rows(shift):
    w = np.zeros((64, 32), np.float32)
    for f in range(64):
        j, r = divmod(f + shift, 4)
        for tap, weight in enumerate(cubic_weights(phase_fraction[r])):
            w[f, j - 2 + tap + (r >= 2) + 8] += weight
    return w


def split_np(w):
    hi = w.astype(BF16)
    lo = (w - hi.astype(np.float32)).astype(BF16)
    return hi, lo


def constants():
    centre, ahead, behind = (refine_rows(s) for s in (0, 1, -1))
    lon = np.zeros((128, 12 * 128), np.float32)
    for s, w in enumerate((centre, ahead, behind)):
        for j in range(4):
            at = (4 * s + j) * 128
            lon[32 * j : 32 * j + 32, at : at + 64] = w.T
            lon[32 * j : 32 * j + 32, at + 64 : at + 128] = w.T
    lh, ll = split_np(lon)
    lon3 = np.concatenate([lh, lh, ll], axis=0)
    first = (np.arange(12 * 128) % 128 < 64)[:, None]
    th, tl = split_np(np.concatenate([lon.T * first, lon.T * ~first], axis=1))
    lont = np.stack([th, tl])
    lat = np.concatenate([centre, ahead, behind], axis=0)
    ah, al = split_np(lat)
    lat3 = np.concatenate([ah, al, ah], axis=1)
    bh, bl = split_np(np.ascontiguousarray(lat.T))
    latt3 = np.concatenate([bh, bl, bh], axis=1)
    ch, cl = split_np(np.ascontiguousarray(centre.T))
    lattc3 = np.concatenate([ch, cl, ch], axis=1)
    sel = np.zeros((512, 256), np.float32)
    for b in range(BANDS):
        for t in range(32):
            y = 16 * b - 8 + t
            if 0 <= y < NYC:
                sel[32 * b + t, y] = 1
    fold = np.zeros((32, 128), np.float32)
    for j in range(4):
        fold[np.arange(32), 32 * j + np.arange(32)] = 1
    return tuple(
        jnp.asarray(v, BF16)
        for v in (lon3, lont, lat3, latt3, lattc3, sel, np.ascontiguousarray(sel.T), fold)
    )


def split(x):
    hi = x.astype(BF16)
    return hi, (x - hi.astype(F32)).astype(BF16)


def dot(a, b):
    return jnp.dot(a, b, preferred_element_type=F32)


def dot_t(a, b):
    return lax.dot_general(a, b, (((1,), (1,)), ((), ())), preferred_element_type=F32)


def kernel(
    c_hbm, m_hbm, lon_hbm, lat_hbm, bal_hbm, inn_hbm, ow_hbm, *rest
):
    consts_hbm, (
        out,
        lonm, latm, bal_in, inn_in, ow_in,
        lon3, lont, lat3, latt3, lattc3, sel, selt, fold,
        gc, gm, ft, pt, pc, ps, pa, pbs, pb, sw, z2, r2, ysc, c3, r3, ct, hl, g4, cgt, gb, wsc, ob, cv,
        bh, bl, latf, ap3, atph, atpl, bal, inn, ow,
        send, recv, local, loads, ready,
    ) = rest[:8], rest[8:]
    me_m, me_b = lax.axis_index("member"), lax.axis_index("band")
    zl, xc = me_m // XC, me_m % XC
    xx, core = xc // 2, xc % 2
    zh, yb = me_b // YB, me_b % YB
    level = (me_b, lax.rem(me_b + BANDS - YB, BANDS))
    outer = (lax.rem(zh + ZH - 1, ZH), lax.rem(zh + 1, ZH))

    def band_peer(i):
        return lax.rem(me_b + 1 + lax.rem(i + 7, BANDS - 1), BANDS)

    def on_band(b):
        return {"member": me_m, "band": b}

    def on_member(m):
        return {"member": m, "band": me_b}

    def x_peer(d):
        return zl * XC + lax.rem(xx + d, XC // 2) * 2 + core

    other = zl * XC + 2 * xx + 1 - core
    east, west = lax.rem(me_m + 1, MEMBERS), lax.rem(me_m + MEMBERS - 1, MEMBERS)

    def zl_peer(d):
        return lax.rem(zl + d, ZL) * XC + xc

    barrier = pltpu.get_barrier_semaphore()

    def greet(device):
        pl.semaphore_signal(barrier, inc=1, device_id=device, device_id_type=MESH)

    def ahead(y):
        return outer[1] * YB + lax.rem(yb + y, YB)

    def behind(y):
        return outer[0] * YB + lax.rem(yb + y, YB)

    def beside(y):
        return zh * YB + lax.rem(yb + y, YB)

    @pl.loop(0, YB)
    def _(y):
        greet(on_band(ahead(y)))
        greet(on_band(behind(y)))

    @pl.loop(1, YB)
    def _(y):
        greet(on_band(beside(y)))

    greet(on_member(east))
    greet(on_member(west))
    greet(on_member(other))

    @pl.loop(1, ZL)
    def _(d):
        greet(on_member(zl_peer(d)))

    @pl.loop(1, XC // 2)
    def _(d):
        greet(on_member(x_peer(d)))

    loaded = [
        pltpu.make_async_copy(src, dst, loads.at[n])
        for n, (src, dst) in enumerate(
            zip(
                (lon_hbm, lat_hbm, bal_hbm, inn_hbm, ow_hbm, *consts_hbm, c_hbm),
                (lonm, latm, bal_in, inn_in, ow_in, lon3, lont, lat3, latt3, lattc3, sel, selt, fold, cv),
            )
        )
    ]
    mine = pl.ds(pl.multiple_of(LAT * yb, LAT), LAT)
    mine_all = pl.ds(pl.multiple_of(LAT * me_b, LAT), LAT)
    own = [
        pltpu.make_async_copy(src.at[:, level[s]], dst.at[s, :, rows], local.at[s, n])
        for s in range(2)
        for n, (src, dst, rows) in enumerate(((c_hbm, gc, mine), (m_hbm, gm, mine_all)))
    ]
    for copy in loaded + own:
        copy.start()
    pl.semaphore_wait(barrier, 3 * YB - 1 + XC // 2 - 1 + ZL - 1 + 3)
    pl.semaphore_signal(ready, inc=1, device_id=on_band(behind(0)), device_id_type=MESH)

    def push(src, dst, ph, device):
        pltpu.make_async_remote_copy(
            src_ref=src, dst_ref=dst, send_sem=send.at[ph], recv_sem=recv.at[ph],
            device_id=device, device_id_type=MESH,
        ).start()

    def wait_for(ref, sem):
        pltpu.make_async_copy(ref, ref, sem).wait()

    def level_at(b, slot):
        return b if slot == 0 else lax.rem(b + BANDS - YB, BANDS)

    def send_members(b, slot, ph):
        push(m_hbm.at[:, level_at(b, slot)], gm.at[slot, :, mine_all], ph, on_band(b))

    def send_controls(b, slot, half):
        rows = pl.ds(pl.multiple_of(BLOCK * half + LAT * yb, LAT), LAT)
        push(c_hbm.at[:, level_at(b, slot)], gc.at[slot, :, rows], slot, on_band(b))

    @pl.loop(0, YB)
    def _(y):
        send_members(ahead(y), 0, 2)
        send_members(behind(y), 1, 3)

    @pl.loop(0, YB)
    def _(y):
        send_controls(ahead(y), 0, 1)
        send_controls(behind(y), 1, 1)

    @pl.loop(1, YB)
    def _(y):
        send_controls(beside(y), 0, 0)
        send_controls(beside(y), 1, 0)

    @pl.loop(0, YB)
    def _(y):
        send_members(behind(y), 0, 4)
        send_members(ahead(y), 1, 5)

    @pl.loop(1, YB)
    def _(y):
        send_members(beside(y), 0, 4)
        send_members(beside(y), 1, 5)

    two = gm.at[0, 0, pl.ds(0, 8 * LAT)]
    seven = gm.at[0, 0, pl.ds(0, 14 * LAT)]

    def block(group):
        return pl.ds(pl.multiple_of(BLOCK * group, BLOCK), BLOCK)

    def relay():
        wait_for(two, recv.at[3])
        rows = block(outer[1])
        push(gm.at[1, :, rows], gm.at[0, :, rows], 6, on_band(outer[0] * YB + yb))
        wait_for(two, recv.at[2])
        rows = block(outer[0])
        push(gm.at[0, :, rows], gm.at[1, :, rows], 7, on_band(outer[1] * YB + yb))

    def prepare():
        for copy in loaded:
            copy.wait()
        for i in range(4):
            rows = pl.ds(128 * i, 128)
            bh[rows, :], bl[rows, :] = split(lonm[rows, :])
        for i in range(2):
            latf[:, pl.ds(128 * i, 128)] = latm[pl.ds(128 * i, 128), :].T
        for s in range(2):
            half = jnp.concatenate([latf[block(zh), :], latf[block(outer[s]), :]], axis=0)
            atph[s], atpl[s] = split(half)
            h, l = split(half.T)
            ap3[s] = jnp.concatenate([h, l, h], axis=1)
        for n in range(5):
            bal[n] = jnp.concatenate([bal_in[n], bal_in[n]], axis=1)
        for p in range(LEVELS // 2):
            inn[p] = jnp.concatenate([inn_in[2 * p], inn_in[2 * p + 1]], axis=1)
            ow[p] = jnp.concatenate([ow_in[2 * p], ow_in[2 * p + 1]], axis=1)
        row = lax.broadcasted_iota(jnp.int32, (64, 128), 0)
        bal[3] = jnp.where((row == 63) & (me_b == BANDS - 1), 0.0, bal[3])
        bal[4] = jnp.where((row == 0) & (me_b == 0), 0.0, bal[4])

    def fields():
        for copy in own:
            copy.wait()
        wait_for(seven, recv.at[0])
        wait_for(seven, recv.at[1])

        @pl.loop(0, 2)
        def _(s):
            @pl.loop(0, 2)
            def _(k):
                ch, cl = split(gc[s, k])
                x = dot_t(ch, bh[...]) + dot_t(cl, bh[...]) + dot_t(ch, bl[...])
                xh, xl = split(x)
                ft[s, k] = dot(ap3[s], jnp.concatenate([xh, xh, xl], axis=0))

    def products(s):
        wait_for(seven, recv.at[4 + s])
        wait_for(two, recv.at[6 + s])
        for i in range(ZL):
            at = pl.ds(128 * i, 128)
            p = (gm[s, 0, :, at] * ft[s, 0, :, at] + gm[s, 1, :, at] * ft[s, 1, :, at]) * SCALE
            pt[s, i] = p.T.reshape(XC // 2, 2, LON, NYC)

        push(pt.at[s, :, :, 1 - core], pc.at[s], 22 + s, on_member(other))

    def reduce_a(s):
        wait_for(pc.at[s], recv.at[22 + s])
        for z in range(ZL):
            ps[s, :, z] = pt[s, z, :, core] + pc[s, z]

        @pl.loop(1, XC // 2)
        def _(d):
            p = lax.rem(xx + d, XC // 2)
            push(ps.at[s, p], pa.at[s, xx], 8 + s, on_member(x_peer(d)))

        pa[s, xx] = ps[s, xx]

    def reduce_b():
        for s in range(2):
            wait_for(pa.at[s, pl.ds(0, XC // 2 - 1)], recv.at[8 + s])
            pbs[:, s] = pa[s, 0] + pa[s, 1] + pa[s, 2] + pa[s, 3]

        @pl.loop(1, ZL)
        def _(d):
            p = zl_peer(d)
            push(pbs.at[p // XC], pb.at[zl], 10, on_member(p))

        pb[zl] = pbs[zl]

    def halo():
        wait_for(pb.at[pl.ds(0, ZL - 1)], recv.at[10])
        sw[:, pl.ds(8, LON)] = pb[0] + pb[1] + pb[2] + pb[3]
        push(sw.at[:, pl.ds(8, 8)], sw.at[:, pl.ds(24, 8)], 11, on_member(west))
        push(sw.at[:, pl.ds(16, 8)], sw.at[:, pl.ds(0, 8)], 12, on_member(east))

    def hand_out():
        wait_for(sw.at[:, pl.ds(24, 8)], recv.at[11])
        wait_for(sw.at[:, pl.ds(0, 8)], recv.at[12])
        w, v = sw[0], sw[1]
        wh, wl = split(jnp.concatenate([w, w, w, w, v, v, v, v], axis=0))
        z = dot_t(sel[...], wh) + dot_t(sel[...], wl)
        group = lax.broadcasted_iota(jnp.int32, (BANDS, 8, 128), 2) // 32
        for s in range(2):
            zs = z[:, 128 * s : 128 * s + 128].reshape(BANDS, 4, 8, 128)
            packed = zs[:, 0]
            for j in range(1, 4):
                packed = jnp.where(group == j, zs[:, j], packed)
            z2[:, s] = packed
        pl.semaphore_wait(ready, 1)

        @pl.loop(0, BANDS - 1)
        def _(i):
            b = band_peer(i)
            push(z2.at[b], r2.at[me_b], 13, on_band(b))

        r2[me_b] = z2[me_b]

    def fine():
        wait_for(r2.at[pl.ds(0, BANDS - 1)], recv.at[13])
        x = jnp.concatenate(
            [
                r2[lev, 0] + r2[(lev + YB) % BANDS, 1]
                for first in range(2)
                for lev in range(first, LEVELS, 2)
            ],
            axis=0,
        )
        xh, xl = split(x)
        y = dot(jnp.concatenate([xh, xl, xh], axis=1), lon3[...])
        left = lax.broadcasted_iota(jnp.int32, (4 * LEVELS, 128), 1) < 64
        for s in range(3):
            for j in range(4):
                at = slice((4 * s + j) * 128, (4 * s + j + 1) * 128)
                pair = jnp.where(left, y[: 4 * LEVELS, at], y[4 * LEVELS :, at])
                for p in range(LEVELS // 2):
                    ysc[s, pl.ds(8 * j, 8), pl.ds(128 * p, 128)] = pair[8 * p : 8 * p + 8]

        def stacked(v):
            h, l = split(v)
            return jnp.concatenate([h, h, l], axis=0)

        v_c = dot(lat3[...], stacked(ysc[0]))
        v_e = dot(lat3[pl.ds(0, 64), :], stacked(ysc[1]))
        v_w = dot(lat3[pl.ds(0, 64), :], stacked(ysc[2]))
        to_c, to_e, to_w = [], [], []
        for p in range(LEVELS // 2):
            at = slice(128 * p, 128 * p + 128)
            image = (
                bal[0] * v_c[0:64, at] + bal[1] * v_e[:, at] + bal[2] * v_w[:, at]
                + bal[3] * v_c[64:128, at] + bal[4] * v_c[128:192, at]
            )
            misfit = ow[p] * (image - inn[p])
            to_c.append(
                jnp.concatenate([bal[0] * misfit, bal[3] * misfit, bal[4] * misfit], axis=0)
            )
            to_e.append(bal[1] * misfit)
            to_w.append(bal[2] * misfit)
        t = (
            dot(latt3[...], stacked(jnp.concatenate(to_c, axis=1))),
            dot(lattc3[...], stacked(jnp.concatenate(to_e, axis=1))),
            dot(lattc3[...], stacked(jnp.concatenate(to_w, axis=1))),
        )
        rows = []
        for p in range(LEVELS // 2):
            rows.append(
                jnp.concatenate(
                    [
                        t[s][8 * j : 8 * j + 8, 128 * p : 128 * p + 128]
                        for s in range(3)
                        for j in range(4)
                    ],
                    axis=1,
                )
            )
        lh, ll = split(jnp.concatenate(rows, axis=0))
        c = dot(lh, lont[0]) + dot(ll, lont[0]) + dot(lh, lont[1])
        for lev in range(LEVELS):
            p, at = lev // 2, slice(128 * (lev % 2), 128 * (lev % 2) + 128)
            c3[lev, 0] = c[8 * p : 8 * p + 8, at]
            c3[(lev + YB) % BANDS, 1] = c[8 * p : 8 * p + 8, at]

        @pl.loop(0, BANDS - 1)
        def _(i):
            b = band_peer(i)
            push(c3.at[b], r3.at[me_b], 14, on_band(b))

        r3[me_b] = c3[me_b]

    def gather_in():
        wait_for(r3.at[pl.ds(0, BANDS - 1)], recv.at[14])
        group = lax.broadcasted_iota(jnp.int32, (BANDS, 8, 128), 2) // 32
        both = []
        for s in range(2):
            r = r3[:, s]
            e = jnp.stack([jnp.where(group == j, r, 0.0) for j in range(4)], axis=1)
            both.append(e.reshape(512, 128))
        eh, el = split(jnp.concatenate(both, axis=1))
        oh, ol = split(dot(selt[...], eh) + dot(selt[...], el))
        for s in range(2):
            at = slice(128 * s, 128 * s + 128)
            ct[s] = dot_t(fold[...], oh[:, at]) + dot_t(fold[...], ol[:, at])
        push(ct.at[:, pl.ds(0, 8)], hl.at[1], 15, on_member(west))
        push(ct.at[:, pl.ds(24, 8)], hl.at[0], 16, on_member(east))

    def spread_b():
        wait_for(hl.at[1], recv.at[15])
        wait_for(hl.at[0], recv.at[16])
        own_part = ct[:, pl.ds(8, LON)] + jnp.concatenate([hl[0], hl[1]], axis=1)
        g4[zl] = own_part * SCALE

        @pl.loop(1, ZL)
        def _(d):
            push(g4.at[zl], g4.at[zl], 17, on_member(zl_peer(d)))

    def spread_a():
        wait_for(g4.at[pl.ds(0, ZL - 1)], recv.at[17])
        for s in range(2):

            @pl.loop(1, XC // 2)
            def _(d):
                push(g4.at[:, s], cgt.at[s, core, xx], 18 + s, on_member(x_peer(d)))

            cgt[s, core, xx] = g4[:, s]

    def spread_core(s):
        wait_for(cgt.at[s, 0, pl.ds(0, XC // 2 - 1)], recv.at[18 + s])
        push(cgt.at[s, core], cgt.at[s, core], 24 + s, on_member(other))

    def weigh(s):
        wait_for(cgt.at[s, 0], recv.at[24 + s])
        for i in range(ZL):
            at = pl.ds(128 * i, 128)
            g = jnp.concatenate(
                [cgt[s, c, x, i] for x in range(XC // 2) for c in range(2)], axis=0
            ).T
            for k in range(2):
                w = gm[s, k, :, at] * g
                h = w.astype(BF16)
                wsc[s, 0, k, :, at] = h
                wsc[s, 1, k, :, at] = (w - h.astype(F32)).astype(BF16)

    def adjoint(s, half, k):
        rows = pl.ds(BLOCK * half, BLOCK)
        ph, plo = atph[s, rows], atpl[s, rows]
        t = dot(ph, wsc[s, 0, k]) + dot(plo, wsc[s, 0, k]) + dot(ph, wsc[s, 1, k])
        th, tl = split(t)
        gb[s, k, rows] = dot(th, bh[...]) + dot(tl, bh[...]) + dot(th, bl[...])

    def give(s, half, k):
        to = (behind, ahead)[s] if half else beside

        @pl.loop(0 if half else 1, YB)
        def _(y):
            rows = pl.ds(pl.multiple_of(BLOCK * half + LAT * lax.rem(yb + y, YB), LAT), LAT)
            push(gb.at[s, k, rows], ob.at[k, level[s]], 20 + s, on_band(to(y)))

        if not half:
            ob[k, level[s]] = gb[s, k, mine, :]

    def finish():
        for s in range(2):
            wait_for(seven, recv.at[20 + s])
        out[...] = ob[...] + cv[...]
        for ph in (0, 1, 4, 5, 20, 21):
            wait_for(seven, send.at[ph])
        for ph in (2, 3, 6, 7):
            wait_for(two, send.at[ph])
        for s in range(2):
            wait_for(pc.at[s], send.at[22 + s])
            wait_for(pc.at[s], send.at[24 + s])
            wait_for(pa.at[s, pl.ds(0, XC // 2 - 1)], send.at[8 + s])
            wait_for(pa.at[s, pl.ds(0, XC // 2 - 1)], send.at[18 + s])
        wait_for(pb.at[pl.ds(0, ZL - 1)], send.at[10])
        wait_for(pb.at[pl.ds(0, ZL - 1)], send.at[17])
        for ph in (11, 12, 15, 16):
            wait_for(hl.at[0], send.at[ph])
        wait_for(r2.at[pl.ds(0, BANDS - 1)], send.at[13])
        wait_for(r3.at[pl.ds(0, BANDS - 1)], send.at[14])

    relay()
    prepare()
    fields()
    products(0)
    products(1)
    reduce_a(0)
    reduce_a(1)
    reduce_b()
    halo()
    hand_out()
    fine()
    gather_in()
    spread_b()
    spread_a()
    spread_core(0)
    spread_core(1)
    weigh(0)
    adjoint(0, 1, 0)
    give(0, 1, 0)
    weigh(1)
    for s, half, k in ((1, 1, 0), (0, 1, 1), (1, 1, 1), (0, 0, 0), (1, 0, 0), (0, 0, 1), (1, 0, 1)):
        adjoint(s, half, k)
        give(s, half, k)
    finish()


def body(controls, members, loc_lon, loc_lat, balance, innovation, obs_weight):
    consts = constants()
    hbm = pl.BlockSpec(memory_space=pl.ANY)
    vmem = pl.BlockSpec(memory_space=pltpu.VMEM)
    f32 = lambda *s: pltpu.VMEM(s, F32)
    b16 = lambda *s: pltpu.VMEM(s, BF16)
    small = (loc_lon, loc_lat, balance, innovation, obs_weight)
    return pl.pallas_call(
        kernel,
        out_shape=jax.ShapeDtypeStruct(controls.shape, F32),
        in_specs=[hbm] * (7 + len(consts)),
        out_specs=vmem,
        scratch_shapes=[pltpu.VMEM(v.shape, v.dtype) for v in (*small, *consts)]
        + [
            f32(2, 2, 2 * BLOCK, NXC),
            f32(2, 2, NYC, NXC),
            f32(2, 2, NYC, NXC),
            f32(2, ZL, XC // 2, 2, LON, NYC),
            f32(2, ZL, XC // 2, LON, NYC),
            f32(2, XC // 2, ZL, LON, NYC),
            f32(2, XC // 2, ZL, LON, NYC),
            f32(ZL, 2, LON, NYC),
            f32(ZL, 2, LON, NYC),
            f32(2, 32, NYC),
            f32(BANDS, 2, 8, 128),
            f32(BANDS, 2, 8, 128),
            f32(3, 32, LEVELS * 64),
            f32(BANDS, 2, 8, 128),
            f32(BANDS, 2, 8, 128),
            f32(2, 32, NYC),
            f32(2, 2, 8, NYC),
            f32(ZL, 2, LON, NYC),
            f32(2, 2, XC // 2, ZL, LON, NYC),
            f32(2, 2, 2 * BLOCK, NXC),
            b16(2, 2, 2, NYC, NXC),
            pltpu.VMEM(controls.shape, F32),
            pltpu.VMEM(controls.shape, F32),
            b16(NXC, NXC), b16(NXC, NXC), f32(NYC, NYC),
            b16(2, NYC, 6 * BLOCK), b16(2, 2 * BLOCK, NYC), b16(2, 2 * BLOCK, NYC),
            f32(5, 64, 128), f32(LEVELS // 2, 64, 128), f32(LEVELS // 2, 64, 128),
            pltpu.SemaphoreType.DMA((26,)),
            pltpu.SemaphoreType.DMA((26,)),
            pltpu.SemaphoreType.DMA((2, 2)),
            pltpu.SemaphoreType.DMA((14,)),
            pltpu.SemaphoreType.REGULAR,
        ],
        compiler_params=pltpu.CompilerParams(
            collective_id=0, has_side_effects=True, vmem_limit_bytes=56 << 20
        ),
        name="gradient",
    )(controls, members, *small, *consts)


def solution(mesh):
    return jax.shard_map(
        body,
        mesh=mesh,
        in_specs=(
            P("member", None, "band", None),
            P("member", None, "band", None),
            P(),
            P(),
            P(None, "band", "member"),
            P(None, "band", "member"),
            P(None, "band", "member"),
        ),
        out_specs=P("member", None, "band", None),
        check_vma=False,
    )
```

```python
import math

import jax
import jax.numpy as jnp
import numpy as np
from jax import lax
from jax.experimental import pallas as pl
from jax.experimental.pallas import tpu as pltpu
from jax.sharding import PartitionSpec as P

MESH = pl.DeviceIdType.MESH
BF16 = jnp.bfloat16
F32 = jnp.float32

phase_fraction = (0.625, 0.875, 0.125, 0.375)

KEN, LEVELS, NYC, NXC = 64, 16, 256, 512
BANDS, MEMBERS, XC, ZL = 16, 32, 8, 4
ZH, YB = 4, 4
BLOCK = NYC // ZH
LAT, LON = NYC // BANDS, NXC // MEMBERS
SCALE = 1.0 / math.sqrt(KEN - 1)


def cubic_weights(fraction):
    return (
        (-(fraction**3) + 2 * fraction**2 - fraction) / 2,
        (3 * fraction**3 - 5 * fraction**2 + 2) / 2,
        (-3 * fraction**3 + 4 * fraction**2 + fraction) / 2,
        (fraction**3 - fraction**2) / 2,
    )


def refine_rows(shift):
    w = np.zeros((64, 32), np.float32)
    for f in range(64):
        j, r = divmod(f + shift, 4)
        for tap, weight in enumerate(cubic_weights(phase_fraction[r])):
            w[f, j - 2 + tap + (r >= 2) + 8] += weight
    return w


def split_np(w):
    hi = w.astype(BF16)
    lo = (w - hi.astype(np.float32)).astype(BF16)
    return hi, lo


def constants():
    centre, ahead, behind = (refine_rows(s) for s in (0, 1, -1))
    lon = np.zeros((128, 12 * 128), np.float32)
    for s, w in enumerate((centre, ahead, behind)):
        for j in range(4):
            at = (4 * s + j) * 128
            lon[32 * j : 32 * j + 32, at : at + 64] = w.T
            lon[32 * j : 32 * j + 32, at + 64 : at + 128] = w.T
    lh, ll = split_np(lon)
    lon3 = np.concatenate([lh, lh, ll], axis=0)
    first = (np.arange(12 * 128) % 128 < 64)[:, None]
    th, tl = split_np(np.concatenate([lon.T * first, lon.T * ~first], axis=1))
    lont = np.stack([th, tl])
    lat = np.concatenate([centre, ahead, behind], axis=0)
    ah, al = split_np(lat)
    lat3 = np.concatenate([ah, al, ah], axis=1)
    bh, bl = split_np(np.ascontiguousarray(lat.T))
    latt3 = np.concatenate([bh, bl, bh], axis=1)
    ch, cl = split_np(np.ascontiguousarray(centre.T))
    lattc3 = np.concatenate([ch, cl, ch], axis=1)
    sel = np.zeros((512, 256), np.float32)
    for b in range(BANDS):
        for t in range(32):
            y = 16 * b - 8 + t
            if 0 <= y < NYC:
                sel[32 * b + t, y] = 1
    fold = np.zeros((32, 128), np.float32)
    for j in range(4):
        fold[np.arange(32), 32 * j + np.arange(32)] = 1
    return tuple(
        jnp.asarray(v, BF16)
        for v in (lon3, lont, lat3, latt3, lattc3, sel, np.ascontiguousarray(sel.T), fold)
    )


def split(x):
    hi = x.astype(BF16)
    return hi, (x - hi.astype(F32)).astype(BF16)


def dot(a, b):
    return jnp.dot(a, b, preferred_element_type=F32)


def dot_t(a, b):
    return lax.dot_general(a, b, (((1,), (1,)), ((), ())), preferred_element_type=F32)


def kernel(
    c_hbm, m_hbm, lon_hbm, lat_hbm, bal_hbm, inn_hbm, ow_hbm, *rest
):
    consts_hbm, (
        out,
        lonm, latm, bal_in, inn_in, ow_in,
        lon3, lont, lat3, latt3, lattc3, sel, selt, fold,
        gc, gm, ft, pt, pc, ps, pa, pbs, pb, sw, z2, r2, ysc, c3, r3, ct, hl, g4, cgt, gb, wsc, ob, cv,
        bh, bl, latf, ap3, atph, atpl, bal, inn, ow,
        send, recv, local, loads, ready,
    ) = rest[:8], rest[8:]
    me_m, me_b = lax.axis_index("member"), lax.axis_index("band")
    zl, xc = me_m // XC, me_m % XC
    xx, core = xc // 2, xc % 2
    zh, yb = me_b // YB, me_b % YB
    level = (me_b, lax.rem(me_b + BANDS - YB, BANDS))
    outer = (lax.rem(zh + ZH - 1, ZH), lax.rem(zh + 1, ZH))

    def band_peer(i):
        return lax.rem(me_b + 1 + lax.rem(i + 7, BANDS - 1), BANDS)

    def on_band(b):
        return {"member": me_m, "band": b}

    def on_member(m):
        return {"member": m, "band": me_b}

    def x_peer(d):
        return zl * XC + lax.rem(xx + d, XC // 2) * 2 + core

    other = zl * XC + 2 * xx + 1 - core
    east, west = lax.rem(me_m + 1, MEMBERS), lax.rem(me_m + MEMBERS - 1, MEMBERS)

    def zl_peer(d):
        return lax.rem(zl + d, ZL) * XC + xc

    barrier = pltpu.get_barrier_semaphore()

    def greet(device):
        pl.semaphore_signal(barrier, inc=1, device_id=device, device_id_type=MESH)

    def ahead(y):
        return outer[1] * YB + lax.rem(yb + y, YB)

    def behind(y):
        return outer[0] * YB + lax.rem(yb + y, YB)

    def beside(y):
        return zh * YB + lax.rem(yb + y, YB)

    @pl.loop(0, YB)
    def _(y):
        greet(on_band(ahead(y)))
        greet(on_band(behind(y)))

    @pl.loop(1, YB)
    def _(y):
        greet(on_band(beside(y)))

    greet(on_member(east))
    greet(on_member(west))
    greet(on_member(other))

    @pl.loop(1, ZL)
    def _(d):
        greet(on_member(zl_peer(d)))

    @pl.loop(1, XC // 2)
    def _(d):
        greet(on_member(x_peer(d)))

    loaded = [
        pltpu.make_async_copy(src, dst, loads.at[n])
        for n, (src, dst) in enumerate(
            zip(
                (lon_hbm, lat_hbm, bal_hbm, inn_hbm, ow_hbm, *consts_hbm, c_hbm),
                (lonm, latm, bal_in, inn_in, ow_in, lon3, lont, lat3, latt3, lattc3, sel, selt, fold, cv),
            )
        )
    ]
    mine = pl.ds(pl.multiple_of(LAT * yb, LAT), LAT)
    mine_all = pl.ds(pl.multiple_of(LAT * me_b, LAT), LAT)
    own = [
        pltpu.make_async_copy(src.at[:, level[s]], dst.at[s, :, rows], local.at[s, n])
        for s in range(2)
        for n, (src, dst, rows) in enumerate(((c_hbm, gc, mine), (m_hbm, gm, mine_all)))
    ]
    for copy in loaded + own:
        copy.start()
    pl.semaphore_wait(barrier, 3 * YB - 1 + XC // 2 - 1 + ZL - 1 + 3)
    pl.semaphore_signal(ready, inc=1, device_id=on_band(behind(0)), device_id_type=MESH)

    def push(src, dst, ph, device):
        pltpu.make_async_remote_copy(
            src_ref=src, dst_ref=dst, send_sem=send.at[ph], recv_sem=recv.at[ph],
            device_id=device, device_id_type=MESH,
        ).start()

    def wait_for(ref, sem):
        pltpu.make_async_copy(ref, ref, sem).wait()

    def level_at(b, slot):
        return b if slot == 0 else lax.rem(b + BANDS - YB, BANDS)

    def send_members(b, slot, ph):
        push(m_hbm.at[:, level_at(b, slot)], gm.at[slot, :, mine_all], ph, on_band(b))

    def send_controls(b, slot, half):
        rows = pl.ds(pl.multiple_of(BLOCK * half + LAT * yb, LAT), LAT)
        push(c_hbm.at[:, level_at(b, slot)], gc.at[slot, :, rows], slot, on_band(b))

    @pl.loop(0, YB)
    def _(y):
        send_members(ahead(y), 0, 2)
        send_members(behind(y), 1, 3)

    def send_far_controls(b, k, ph):
        rows = pl.ds(pl.multiple_of(BLOCK + LAT * yb, LAT), LAT)
        push(c_hbm.at[k, level_at(b, 1)], gc.at[1, k, rows], ph, on_band(b))

    @pl.loop(0, YB)
    def _(y):
        send_controls(ahead(y), 0, 1)
        send_far_controls(behind(y), 0, 1)

    @pl.loop(1, YB)
    def _(y):
        send_controls(beside(y), 0, 0)
        send_controls(beside(y), 1, 0)

    @pl.loop(0, YB)
    def _(y):
        send_members(behind(y), 0, 4)
        send_members(ahead(y), 1, 5)

    @pl.loop(1, YB)
    def _(y):
        send_members(beside(y), 0, 4)
        send_members(beside(y), 1, 5)

    two = gm.at[0, 0, pl.ds(0, 8 * LAT)]
    seven = gm.at[0, 0, pl.ds(0, 14 * LAT)]
    five = gm.at[0, 0, pl.ds(0, 10 * LAT)]
    four = gm.at[0, 0, pl.ds(0, 4 * LAT)]

    def block(group):
        return pl.ds(pl.multiple_of(BLOCK * group, BLOCK), BLOCK)

    def relay():
        wait_for(two, recv.at[3])
        rows = block(outer[1])
        push(gm.at[1, :, rows], gm.at[0, :, rows], 6, on_band(outer[0] * YB + yb))

        @pl.loop(0, YB)
        def _(y):
            send_far_controls(behind(y), 1, 26)

        wait_for(two, recv.at[2])
        rows = block(outer[0])
        push(gm.at[0, :, rows], gm.at[1, :, rows], 7, on_band(outer[1] * YB + yb))

    def prepare():
        for copy in loaded:
            copy.wait()
        for i in range(4):
            rows = pl.ds(128 * i, 128)
            bh[rows, :], bl[rows, :] = split(lonm[rows, :])
        for i in range(2):
            latf[:, pl.ds(128 * i, 128)] = latm[pl.ds(128 * i, 128), :].T
        for s in range(2):
            half = jnp.concatenate([latf[block(zh), :], latf[block(outer[s]), :]], axis=0)
            atph[s], atpl[s] = split(half)
            h, l = split(half.T)
            ap3[s] = jnp.concatenate([h, l, h], axis=1)
        for n in range(5):
            bal[n] = jnp.concatenate([bal_in[n], bal_in[n]], axis=1)
        for p in range(LEVELS // 2):
            inn[p] = jnp.concatenate([inn_in[2 * p], inn_in[2 * p + 1]], axis=1)
            ow[p] = jnp.concatenate([ow_in[2 * p], ow_in[2 * p + 1]], axis=1)
        row = lax.broadcasted_iota(jnp.int32, (64, 128), 0)
        bal[3] = jnp.where((row == 63) & (me_b == BANDS - 1), 0.0, bal[3])
        bal[4] = jnp.where((row == 0) & (me_b == 0), 0.0, bal[4])

    def field(s, k):
        ch, cl = split(gc[s, k])
        x = dot_t(ch, bh[...]) + dot_t(cl, bh[...]) + dot_t(ch, bl[...])
        xh, xl = split(x)
        ft[s, k] = dot(ap3[s], jnp.concatenate([xh, xh, xl], axis=0))

    def fields():
        for copy in own:
            copy.wait()
        wait_for(seven, recv.at[0])
        wait_for(five, recv.at[1])
        field(0, 0)
        field(0, 1)
        field(1, 0)

    def last_field():
        wait_for(four, recv.at[26])
        field(1, 1)

    def products(s):
        wait_for(seven, recv.at[4 + s])
        wait_for(two, recv.at[6 + s])
        for i in range(ZL):
            at = pl.ds(128 * i, 128)
            p = (gm[s, 0, :, at] * ft[s, 0, :, at] + gm[s, 1, :, at] * ft[s, 1, :, at]) * SCALE
            pt[s, i] = p.T.reshape(XC // 2, 2, LON, NYC)

        push(pt.at[s, :, :, 1 - core], pc.at[s], 22 + s, on_member(other))

    def reduce_a(s):
        wait_for(pc.at[s], recv.at[22 + s])
        for z in range(ZL):
            ps[s, :, z] = pt[s, z, :, core] + pc[s, z]

        @pl.loop(1, XC // 2)
        def _(d):
            p = lax.rem(xx + d, XC // 2)
            push(ps.at[s, p], pa.at[s, xx], 8 + s, on_member(x_peer(d)))

        pa[s, xx] = ps[s, xx]

    def reduce_b():
        for s in range(2):
            wait_for(pa.at[s, pl.ds(0, XC // 2 - 1)], recv.at[8 + s])
            pbs[:, s] = pa[s, 0] + pa[s, 1] + pa[s, 2] + pa[s, 3]

        @pl.loop(1, ZL)
        def _(d):
            p = zl_peer(d)
            push(pbs.at[p // XC], pb.at[zl], 10, on_member(p))

        pb[zl] = pbs[zl]

    def halo():
        wait_for(pb.at[pl.ds(0, ZL - 1)], recv.at[10])
        sw[:, pl.ds(8, LON)] = pb[0] + pb[1] + pb[2] + pb[3]
        push(sw.at[:, pl.ds(8, 8)], sw.at[:, pl.ds(24, 8)], 11, on_member(west))
        push(sw.at[:, pl.ds(16, 8)], sw.at[:, pl.ds(0, 8)], 12, on_member(east))

    def hand_out():
        wait_for(sw.at[:, pl.ds(24, 8)], recv.at[11])
        wait_for(sw.at[:, pl.ds(0, 8)], recv.at[12])
        w, v = sw[0], sw[1]
        wh, wl = split(jnp.concatenate([w, w, w, w, v, v, v, v], axis=0))
        z = dot_t(sel[...], wh) + dot_t(sel[...], wl)
        group = lax.broadcasted_iota(jnp.int32, (BANDS, 8, 128), 2) // 32
        for s in range(2):
            zs = z[:, 128 * s : 128 * s + 128].reshape(BANDS, 4, 8, 128)
            packed = zs[:, 0]
            for j in range(1, 4):
                packed = jnp.where(group == j, zs[:, j], packed)
            z2[:, s] = packed
        pl.semaphore_wait(ready, 1)

        @pl.loop(0, BANDS - 1)
        def _(i):
            b = band_peer(i)
            push(z2.at[b], r2.at[me_b], 13, on_band(b))

        r2[me_b] = z2[me_b]

    def fine():
        wait_for(r2.at[pl.ds(0, BANDS - 1)], recv.at[13])
        x = jnp.concatenate(
            [
                r2[lev, 0] + r2[(lev + YB) % BANDS, 1]
                for first in range(2)
                for lev in range(first, LEVELS, 2)
            ],
            axis=0,
        )
        xh, xl = split(x)
        y = dot(jnp.concatenate([xh, xl, xh], axis=1), lon3[...])
        left = lax.broadcasted_iota(jnp.int32, (4 * LEVELS, 128), 1) < 64
        for s in range(3):
            for j in range(4):
                at = slice((4 * s + j) * 128, (4 * s + j + 1) * 128)
                pair = jnp.where(left, y[: 4 * LEVELS, at], y[4 * LEVELS :, at])
                for p in range(LEVELS // 2):
                    ysc[s, pl.ds(8 * j, 8), pl.ds(128 * p, 128)] = pair[8 * p : 8 * p + 8]

        def stacked(v):
            h, l = split(v)
            return jnp.concatenate([h, h, l], axis=0)

        v_c = dot(lat3[...], stacked(ysc[0]))
        v_e = dot(lat3[pl.ds(0, 64), :], stacked(ysc[1]))
        v_w = dot(lat3[pl.ds(0, 64), :], stacked(ysc[2]))
        to_c, to_e, to_w = [], [], []
        for p in range(LEVELS // 2):
            at = slice(128 * p, 128 * p + 128)
            image = (
                bal[0] * v_c[0:64, at] + bal[1] * v_e[:, at] + bal[2] * v_w[:, at]
                + bal[3] * v_c[64:128, at] + bal[4] * v_c[128:192, at]
            )
            misfit = ow[p] * (image - inn[p])
            to_c.append(
                jnp.concatenate([bal[0] * misfit, bal[3] * misfit, bal[4] * misfit], axis=0)
            )
            to_e.append(bal[1] * misfit)
            to_w.append(bal[2] * misfit)
        t = (
            dot(latt3[...], stacked(jnp.concatenate(to_c, axis=1))),
            dot(lattc3[...], stacked(jnp.concatenate(to_e, axis=1))),
            dot(lattc3[...], stacked(jnp.concatenate(to_w, axis=1))),
        )
        rows = []
        for p in range(LEVELS // 2):
            rows.append(
                jnp.concatenate(
                    [
                        t[s][8 * j : 8 * j + 8, 128 * p : 128 * p + 128]
                        for s in range(3)
                        for j in range(4)
                    ],
                    axis=1,
                )
            )
        lh, ll = split(jnp.concatenate(rows, axis=0))
        c = dot(lh, lont[0]) + dot(ll, lont[0]) + dot(lh, lont[1])
        for lev in range(LEVELS):
            p, at = lev // 2, slice(128 * (lev % 2), 128 * (lev % 2) + 128)
            c3[lev, 0] = c[8 * p : 8 * p + 8, at]
            c3[(lev + YB) % BANDS, 1] = c[8 * p : 8 * p + 8, at]

        @pl.loop(0, BANDS - 1)
        def _(i):
            b = band_peer(i)
            push(c3.at[b], r3.at[me_b], 14, on_band(b))

        r3[me_b] = c3[me_b]

    def gather_in():
        wait_for(r3.at[pl.ds(0, BANDS - 1)], recv.at[14])
        group = lax.broadcasted_iota(jnp.int32, (BANDS, 8, 128), 2) // 32
        both = []
        for s in range(2):
            r = r3[:, s]
            e = jnp.stack([jnp.where(group == j, r, 0.0) for j in range(4)], axis=1)
            both.append(e.reshape(512, 128))
        eh, el = split(jnp.concatenate(both, axis=1))
        oh, ol = split(dot(selt[...], eh) + dot(selt[...], el))
        for s in range(2):
            at = slice(128 * s, 128 * s + 128)
            ct[s] = dot_t(fold[...], oh[:, at]) + dot_t(fold[...], ol[:, at])
        push(ct.at[:, pl.ds(0, 8)], hl.at[1], 15, on_member(west))
        push(ct.at[:, pl.ds(24, 8)], hl.at[0], 16, on_member(east))

    def spread_b():
        wait_for(hl.at[1], recv.at[15])
        wait_for(hl.at[0], recv.at[16])
        own_part = ct[:, pl.ds(8, LON)] + jnp.concatenate([hl[0], hl[1]], axis=1)
        g4[zl] = own_part * SCALE

        @pl.loop(1, ZL)
        def _(d):
            push(g4.at[zl], g4.at[zl], 17, on_member(zl_peer(d)))

    def spread_a():
        wait_for(g4.at[pl.ds(0, ZL - 1)], recv.at[17])
        for s in range(2):

            @pl.loop(1, XC // 2)
            def _(d):
                push(g4.at[:, s], cgt.at[s, core, xx], 18 + s, on_member(x_peer(d)))

            cgt[s, core, xx] = g4[:, s]

    def spread_core(s):
        wait_for(cgt.at[s, 0, pl.ds(0, XC // 2 - 1)], recv.at[18 + s])
        push(cgt.at[s, core], cgt.at[s, core], 24 + s, on_member(other))

    def weigh(s):
        wait_for(cgt.at[s, 0], recv.at[24 + s])
        for i in range(ZL):
            at = pl.ds(128 * i, 128)
            g = jnp.concatenate(
                [cgt[s, c, x, i] for x in range(XC // 2) for c in range(2)], axis=0
            ).T
            for k in range(2):
                w = gm[s, k, :, at] * g
                h = w.astype(BF16)
                wsc[s, 0, k, :, at] = h
                wsc[s, 1, k, :, at] = (w - h.astype(F32)).astype(BF16)

    def adjoint(s, half, k):
        rows = pl.ds(BLOCK * half, BLOCK)
        ph, plo = atph[s, rows], atpl[s, rows]
        t = dot(ph, wsc[s, 0, k]) + dot(plo, wsc[s, 0, k]) + dot(ph, wsc[s, 1, k])
        th, tl = split(t)
        gb[s, k, rows] = dot(th, bh[...]) + dot(tl, bh[...]) + dot(th, bl[...])

    def give(s, half, k):
        to = (behind, ahead)[s] if half else beside

        @pl.loop(0 if half else 1, YB)
        def _(y):
            rows = pl.ds(pl.multiple_of(BLOCK * half + LAT * lax.rem(yb + y, YB), LAT), LAT)
            push(gb.at[s, k, rows], ob.at[k, level[s]], 20 + s, on_band(to(y)))

        if not half:
            ob[k, level[s]] = gb[s, k, mine, :]

    def finish():
        for s in range(2):
            wait_for(seven, recv.at[20 + s])
        out[...] = ob[...] + cv[...]
        for ph in (0, 4, 5, 20, 21):
            wait_for(seven, send.at[ph])
        wait_for(five, send.at[1])
        wait_for(four, send.at[26])
        for ph in (2, 3, 6, 7):
            wait_for(two, send.at[ph])
        for s in range(2):
            wait_for(pc.at[s], send.at[22 + s])
            wait_for(pc.at[s], send.at[24 + s])
            wait_for(pa.at[s, pl.ds(0, XC // 2 - 1)], send.at[8 + s])
            wait_for(pa.at[s, pl.ds(0, XC // 2 - 1)], send.at[18 + s])
        wait_for(pb.at[pl.ds(0, ZL - 1)], send.at[10])
        wait_for(pb.at[pl.ds(0, ZL - 1)], send.at[17])
        for ph in (11, 12, 15, 16):
            wait_for(hl.at[0], send.at[ph])
        wait_for(r2.at[pl.ds(0, BANDS - 1)], send.at[13])
        wait_for(r3.at[pl.ds(0, BANDS - 1)], send.at[14])

    relay()
    prepare()
    fields()
    products(0)
    reduce_a(0)
    last_field()
    products(1)
    reduce_a(1)
    reduce_b()
    halo()
    hand_out()
    fine()
    gather_in()
    spread_b()
    spread_a()
    spread_core(0)
    spread_core(1)
    weigh(0)
    adjoint(0, 1, 0)
    give(0, 1, 0)
    weigh(1)
    for s, half, k in ((1, 1, 0), (0, 1, 1), (1, 1, 1), (0, 0, 0), (1, 0, 0), (0, 0, 1), (1, 0, 1)):
        adjoint(s, half, k)
        give(s, half, k)
    finish()


def body(controls, members, loc_lon, loc_lat, balance, innovation, obs_weight):
    consts = constants()
    hbm = pl.BlockSpec(memory_space=pl.ANY)
    vmem = pl.BlockSpec(memory_space=pltpu.VMEM)
    f32 = lambda *s: pltpu.VMEM(s, F32)
    b16 = lambda *s: pltpu.VMEM(s, BF16)
    small = (loc_lon, loc_lat, balance, innovation, obs_weight)
    return pl.pallas_call(
        kernel,
        out_shape=jax.ShapeDtypeStruct(controls.shape, F32),
        in_specs=[hbm] * (7 + len(consts)),
        out_specs=vmem,
        scratch_shapes=[pltpu.VMEM(v.shape, v.dtype) for v in (*small, *consts)]
        + [
            f32(2, 2, 2 * BLOCK, NXC),
            f32(2, 2, NYC, NXC),
            f32(2, 2, NYC, NXC),
            f32(2, ZL, XC // 2, 2, LON, NYC),
            f32(2, ZL, XC // 2, LON, NYC),
            f32(2, XC // 2, ZL, LON, NYC),
            f32(2, XC // 2, ZL, LON, NYC),
            f32(ZL, 2, LON, NYC),
            f32(ZL, 2, LON, NYC),
            f32(2, 32, NYC),
            f32(BANDS, 2, 8, 128),
            f32(BANDS, 2, 8, 128),
            f32(3, 32, LEVELS * 64),
            f32(BANDS, 2, 8, 128),
            f32(BANDS, 2, 8, 128),
            f32(2, 32, NYC),
            f32(2, 2, 8, NYC),
            f32(ZL, 2, LON, NYC),
            f32(2, 2, XC // 2, ZL, LON, NYC),
            f32(2, 2, 2 * BLOCK, NXC),
            b16(2, 2, 2, NYC, NXC),
            pltpu.VMEM(controls.shape, F32),
            pltpu.VMEM(controls.shape, F32),
            b16(NXC, NXC), b16(NXC, NXC), f32(NYC, NYC),
            b16(2, NYC, 6 * BLOCK), b16(2, 2 * BLOCK, NYC), b16(2, 2 * BLOCK, NYC),
            f32(5, 64, 128), f32(LEVELS // 2, 64, 128), f32(LEVELS // 2, 64, 128),
            pltpu.SemaphoreType.DMA((27,)),
            pltpu.SemaphoreType.DMA((27,)),
            pltpu.SemaphoreType.DMA((2, 2)),
            pltpu.SemaphoreType.DMA((14,)),
            pltpu.SemaphoreType.REGULAR,
        ],
        compiler_params=pltpu.CompilerParams(
            collective_id=0, has_side_effects=True, vmem_limit_bytes=56 << 20
        ),
        name="gradient",
    )(controls, members, *small, *consts)


def solution(mesh):
    return jax.shard_map(
        body,
        mesh=mesh,
        in_specs=(
            P("member", None, "band", None),
            P("member", None, "band", None),
            P(),
            P(),
            P(None, "band", "member"),
            P(None, "band", "member"),
            P(None, "band", "member"),
        ),
        out_specs=P("member", None, "band", None),
        check_vma=False,
    )
```

```python
import math

import jax
import jax.numpy as jnp
import numpy as np
from jax import lax
from jax.experimental import pallas as pl
from jax.experimental.pallas import tpu as pltpu
from jax.sharding import PartitionSpec as P

MESH = pl.DeviceIdType.MESH
BF16 = jnp.bfloat16
F32 = jnp.float32

phase_fraction = (0.625, 0.875, 0.125, 0.375)

KEN, LEVELS, NYC, NXC = 64, 16, 256, 512
BANDS, MEMBERS, XC, ZL = 16, 32, 8, 4
ZH, YB = 4, 4
BLOCK = NYC // ZH
LAT, LON = NYC // BANDS, NXC // MEMBERS
SCALE = 1.0 / math.sqrt(KEN - 1)


def cubic_weights(fraction):
    return (
        (-(fraction**3) + 2 * fraction**2 - fraction) / 2,
        (3 * fraction**3 - 5 * fraction**2 + 2) / 2,
        (-3 * fraction**3 + 4 * fraction**2 + fraction) / 2,
        (fraction**3 - fraction**2) / 2,
    )


def refine_rows(shift):
    w = np.zeros((64, 32), np.float32)
    for f in range(64):
        j, r = divmod(f + shift, 4)
        for tap, weight in enumerate(cubic_weights(phase_fraction[r])):
            w[f, j - 2 + tap + (r >= 2) + 8] += weight
    return w


def split_np(w):
    hi = w.astype(BF16)
    lo = (w - hi.astype(np.float32)).astype(BF16)
    return hi, lo


def constants():
    centre, ahead, behind = (refine_rows(s) for s in (0, 1, -1))
    lon = np.zeros((128, 12 * 128), np.float32)
    for s, w in enumerate((centre, ahead, behind)):
        for j in range(4):
            at = (4 * s + j) * 128
            lon[32 * j : 32 * j + 32, at : at + 64] = w.T
            lon[32 * j : 32 * j + 32, at + 64 : at + 128] = w.T
    lh, ll = split_np(lon)
    lon3 = np.concatenate([lh, lh, ll], axis=0)
    first = (np.arange(12 * 128) % 128 < 64)[:, None]
    th, tl = split_np(np.concatenate([lon.T * first, lon.T * ~first], axis=1))
    lont = np.stack([th, tl])
    lat = np.concatenate([centre, ahead, behind], axis=0)
    ah, al = split_np(lat)
    lat3 = np.concatenate([ah, al, ah], axis=1)
    bh, bl = split_np(np.ascontiguousarray(lat.T))
    latt3 = np.concatenate([bh, bl, bh], axis=1)
    ch, cl = split_np(np.ascontiguousarray(centre.T))
    lattc3 = np.concatenate([ch, cl, ch], axis=1)
    sel = np.zeros((512, 256), np.float32)
    for b in range(BANDS):
        for t in range(32):
            y = 16 * b - 8 + t
            if 0 <= y < NYC:
                sel[32 * b + t, y] = 1
    fold = np.zeros((32, 128), np.float32)
    for j in range(4):
        fold[np.arange(32), 32 * j + np.arange(32)] = 1
    return tuple(
        jnp.asarray(v, BF16)
        for v in (lon3, lont, lat3, latt3, lattc3, sel, np.ascontiguousarray(sel.T), fold)
    )


def split(x):
    hi = x.astype(BF16)
    return hi, (x - hi.astype(F32)).astype(BF16)


def dot(a, b):
    return jnp.dot(a, b, preferred_element_type=F32)


def dot_t(a, b):
    return lax.dot_general(a, b, (((1,), (1,)), ((), ())), preferred_element_type=F32)


def kernel(
    c_hbm, m_hbm, lon_hbm, lat_hbm, bal_hbm, inn_hbm, ow_hbm, *rest
):
    consts_hbm, (
        out,
        lonm, latm, bal_in, inn_in, ow_in,
        lon3, lont, lat3, latt3, lattc3, sel, selt, fold,
        gc, gm, ft, pt, pc, ps, pa, pbs, pb, sw, z2, r2, ysc, c3, r3, ct, hl, g4, cgt, gb, wsc, ob, cv,
        bh, bl, latf, ap3, atph, atpl, bal, inn, ow,
        send, recv, local, loads, ready,
    ) = rest[:8], rest[8:]
    me_m, me_b = lax.axis_index("member"), lax.axis_index("band")
    zl, xc = me_m // XC, me_m % XC
    xx, core = xc // 2, xc % 2
    zh, yb = me_b // YB, me_b % YB
    level = (me_b, lax.rem(me_b + BANDS - YB, BANDS))
    outer = (lax.rem(zh + ZH - 1, ZH), lax.rem(zh + 1, ZH))

    def band_peer(i):
        return lax.rem(me_b + 1 + lax.rem(i + 7, BANDS - 1), BANDS)

    def on_band(b):
        return {"member": me_m, "band": b}

    def on_member(m):
        return {"member": m, "band": me_b}

    def x_peer(d):
        return zl * XC + lax.rem(xx + d, XC // 2) * 2 + core

    other = zl * XC + 2 * xx + 1 - core
    east, west = lax.rem(me_m + 1, MEMBERS), lax.rem(me_m + MEMBERS - 1, MEMBERS)

    def zl_peer(d):
        return lax.rem(zl + d, ZL) * XC + xc

    barrier = pltpu.get_barrier_semaphore()

    def greet(device):
        pl.semaphore_signal(barrier, inc=1, device_id=device, device_id_type=MESH)

    def ahead(y):
        return outer[1] * YB + lax.rem(yb + y, YB)

    def behind(y):
        return outer[0] * YB + lax.rem(yb + y, YB)

    def beside(y):
        return zh * YB + lax.rem(yb + y, YB)

    @pl.loop(0, YB)
    def _(y):
        greet(on_band(ahead(y)))
        greet(on_band(behind(y)))

    @pl.loop(1, YB)
    def _(y):
        greet(on_band(beside(y)))

    greet(on_member(east))
    greet(on_member(west))
    greet(on_member(other))

    @pl.loop(1, ZL)
    def _(d):
        greet(on_member(zl_peer(d)))

    @pl.loop(1, XC // 2)
    def _(d):
        greet(on_member(x_peer(d)))

    loaded = [
        pltpu.make_async_copy(src, dst, loads.at[n])
        for n, (src, dst) in enumerate(
            zip(
                (lon_hbm, lat_hbm, bal_hbm, inn_hbm, ow_hbm, *consts_hbm, c_hbm),
                (lonm, latm, bal_in, inn_in, ow_in, lon3, lont, lat3, latt3, lattc3, sel, selt, fold, cv),
            )
        )
    ]
    mine = pl.ds(pl.multiple_of(LAT * yb, LAT), LAT)
    mine_all = pl.ds(pl.multiple_of(LAT * me_b, LAT), LAT)
    own = [
        pltpu.make_async_copy(src.at[:, level[s]], dst.at[s, :, rows], local.at[s, n])
        for s in range(2)
        for n, (src, dst, rows) in enumerate(((c_hbm, gc, mine), (m_hbm, gm, mine_all)))
    ]
    for copy in loaded + own:
        copy.start()
    pl.semaphore_wait(barrier, 3 * YB - 1 + XC // 2 - 1 + ZL - 1 + 3)
    pl.semaphore_signal(ready, inc=1, device_id=on_band(behind(0)), device_id_type=MESH)

    def push(src, dst, ph, device):
        pltpu.make_async_remote_copy(
            src_ref=src, dst_ref=dst, send_sem=send.at[ph], recv_sem=recv.at[ph],
            device_id=device, device_id_type=MESH,
        ).start()

    def wait_for(ref, sem):
        pltpu.make_async_copy(ref, ref, sem).wait()

    def level_at(b, slot):
        return b if slot == 0 else lax.rem(b + BANDS - YB, BANDS)

    def send_members(b, slot, ph):
        push(m_hbm.at[:, level_at(b, slot)], gm.at[slot, :, mine_all], ph, on_band(b))

    def send_controls(b, slot, half):
        rows = pl.ds(pl.multiple_of(BLOCK * half + LAT * yb, LAT), LAT)
        push(c_hbm.at[:, level_at(b, slot)], gc.at[slot, :, rows], slot, on_band(b))

    @pl.loop(0, YB)
    def _(y):
        send_members(ahead(y), 0, 2)
        send_members(behind(y), 1, 3)

    @pl.loop(0, YB)
    def _(y):
        send_controls(ahead(y), 0, 1)
        send_controls(behind(y), 1, 1)

    @pl.loop(1, YB)
    def _(y):
        send_controls(beside(y), 0, 0)
        send_controls(beside(y), 1, 0)

    @pl.loop(0, YB)
    def _(y):
        send_members(behind(y), 0, 4)
        send_members(ahead(y), 1, 5)

    @pl.loop(1, YB)
    def _(y):
        send_members(beside(y), 0, 4)
        send_members(beside(y), 1, 5)

    two = gm.at[0, 0, pl.ds(0, 8 * LAT)]
    seven = gm.at[0, 0, pl.ds(0, 14 * LAT)]

    def block(group):
        return pl.ds(pl.multiple_of(BLOCK * group, BLOCK), BLOCK)

    def relay():
        wait_for(two, recv.at[3])
        rows = block(outer[1])
        push(gm.at[1, :, rows], gm.at[0, :, rows], 6, on_band(outer[0] * YB + yb))
        wait_for(two, recv.at[2])
        rows = block(outer[0])
        push(gm.at[0, :, rows], gm.at[1, :, rows], 7, on_band(outer[1] * YB + yb))

    def prepare():
        for copy in loaded:
            copy.wait()
        for i in range(4):
            rows = pl.ds(128 * i, 128)
            bh[rows, :], bl[rows, :] = split(lonm[rows, :])
        for i in range(2):
            latf[:, pl.ds(128 * i, 128)] = latm[pl.ds(128 * i, 128), :].T
        for s in range(2):
            half = jnp.concatenate([latf[block(zh), :], latf[block(outer[s]), :]], axis=0)
            atph[s], atpl[s] = split(half)
            h, l = split(half.T)
            ap3[s] = jnp.concatenate([h, l, h], axis=1)
        for n in range(5):
            bal[n] = jnp.concatenate([bal_in[n], bal_in[n]], axis=1)
        for p in range(LEVELS // 2):
            inn[p] = jnp.concatenate([inn_in[2 * p], inn_in[2 * p + 1]], axis=1)
            ow[p] = jnp.concatenate([ow_in[2 * p], ow_in[2 * p + 1]], axis=1)
        row = lax.broadcasted_iota(jnp.int32, (64, 128), 0)
        bal[3] = jnp.where((row == 63) & (me_b == BANDS - 1), 0.0, bal[3])
        bal[4] = jnp.where((row == 0) & (me_b == 0), 0.0, bal[4])

    def fields():
        for copy in own:
            copy.wait()
        wait_for(seven, recv.at[0])
        wait_for(seven, recv.at[1])

        @pl.loop(0, 2)
        def _(s):
            @pl.loop(0, 2)
            def _(k):
                ch, cl = split(gc[s, k])
                x = dot_t(ch, bh[...]) + dot_t(cl, bh[...]) + dot_t(ch, bl[...])
                xh, xl = split(x)
                ft[s, k] = dot(ap3[s], jnp.concatenate([xh, xh, xl], axis=0))

    def products(s):
        wait_for(seven, recv.at[4 + s])
        wait_for(two, recv.at[6 + s])
        for i in range(ZL):
            at = pl.ds(128 * i, 128)
            p = (gm[s, 0, :, at] * ft[s, 0, :, at] + gm[s, 1, :, at] * ft[s, 1, :, at]) * SCALE
            pt[s, i] = p.T.reshape(XC // 2, 2, LON, NYC)

        push(pt.at[s, :, :, 1 - core], pc.at[s], 22 + s, on_member(other))

    def reduce_a(s):
        wait_for(pc.at[s], recv.at[22 + s])
        for z in range(ZL):
            ps[s, :, z] = pt[s, z, :, core] + pc[s, z]

        @pl.loop(1, XC // 2)
        def _(d):
            p = lax.rem(xx + d, XC // 2)
            push(ps.at[s, p], pa.at[s, xx], 8 + s, on_member(x_peer(d)))

        pa[s, xx] = ps[s, xx]

    def reduce_b():
        for s in range(2):
            wait_for(pa.at[s, pl.ds(0, XC // 2 - 1)], recv.at[8 + s])
            pbs[:, s] = pa[s, 0] + pa[s, 1] + pa[s, 2] + pa[s, 3]

        @pl.loop(1, ZL)
        def _(d):
            p = zl_peer(d)
            push(pbs.at[p // XC], pb.at[zl], 10, on_member(p))

        pb[zl] = pbs[zl]

    def halo():
        wait_for(pb.at[pl.ds(0, ZL - 1)], recv.at[10])
        sw[:, pl.ds(8, LON)] = pb[0] + pb[1] + pb[2] + pb[3]
        push(sw.at[:, pl.ds(8, 8)], sw.at[:, pl.ds(24, 8)], 11, on_member(west))
        push(sw.at[:, pl.ds(16, 8)], sw.at[:, pl.ds(0, 8)], 12, on_member(east))

    def hand_out():
        wait_for(sw.at[:, pl.ds(24, 8)], recv.at[11])
        wait_for(sw.at[:, pl.ds(0, 8)], recv.at[12])
        w, v = sw[0], sw[1]
        wh, wl = split(jnp.concatenate([w, w, w, w, v, v, v, v], axis=0))
        z = dot_t(sel[...], wh) + dot_t(sel[...], wl)
        group = lax.broadcasted_iota(jnp.int32, (BANDS, 8, 128), 2) // 32
        for s in range(2):
            zs = z[:, 128 * s : 128 * s + 128].reshape(BANDS, 4, 8, 128)
            packed = zs[:, 0]
            for j in range(1, 4):
                packed = jnp.where(group == j, zs[:, j], packed)
            z2[:, s] = packed
        pl.semaphore_wait(ready, 1)

        @pl.loop(0, BANDS - 1)
        def _(i):
            b = band_peer(i)
            push(z2.at[b], r2.at[me_b], 13, on_band(b))

        r2[me_b] = z2[me_b]

    def fine():
        wait_for(r2.at[pl.ds(0, BANDS - 1)], recv.at[13])
        x = jnp.concatenate(
            [
                r2[lev, 0] + r2[(lev + YB) % BANDS, 1]
                for first in range(2)
                for lev in range(first, LEVELS, 2)
            ],
            axis=0,
        )
        xh, xl = split(x)
        y = dot(jnp.concatenate([xh, xl, xh], axis=1), lon3[...])
        left = lax.broadcasted_iota(jnp.int32, (4 * LEVELS, 128), 1) < 64
        for s in range(3):
            for j in range(4):
                at = slice((4 * s + j) * 128, (4 * s + j + 1) * 128)
                pair = jnp.where(left, y[: 4 * LEVELS, at], y[4 * LEVELS :, at])
                for p in range(LEVELS // 2):
                    ysc[s, pl.ds(8 * j, 8), pl.ds(128 * p, 128)] = pair[8 * p : 8 * p + 8]

        def stacked(v):
            h, l = split(v)
            return jnp.concatenate([h, h, l], axis=0)

        v_c = dot(lat3[...], stacked(ysc[0]))
        v_e = dot(lat3[pl.ds(0, 64), :], stacked(ysc[1]))
        v_w = dot(lat3[pl.ds(0, 64), :], stacked(ysc[2]))
        to_c, to_e, to_w = [], [], []
        for p in range(LEVELS // 2):
            at = slice(128 * p, 128 * p + 128)
            image = (
                bal[0] * v_c[0:64, at] + bal[1] * v_e[:, at] + bal[2] * v_w[:, at]
                + bal[3] * v_c[64:128, at] + bal[4] * v_c[128:192, at]
            )
            misfit = ow[p] * (image - inn[p])
            to_c.append(
                jnp.concatenate([bal[0] * misfit, bal[3] * misfit, bal[4] * misfit], axis=0)
            )
            to_e.append(bal[1] * misfit)
            to_w.append(bal[2] * misfit)
        t = (
            dot(latt3[...], stacked(jnp.concatenate(to_c, axis=1))),
            dot(lattc3[...], stacked(jnp.concatenate(to_e, axis=1))),
            dot(lattc3[...], stacked(jnp.concatenate(to_w, axis=1))),
        )
        rows = []
        for p in range(LEVELS // 2):
            rows.append(
                jnp.concatenate(
                    [
                        t[s][8 * j : 8 * j + 8, 128 * p : 128 * p + 128]
                        for s in range(3)
                        for j in range(4)
                    ],
                    axis=1,
                )
            )
        lh, ll = split(jnp.concatenate(rows, axis=0))
        c = dot(lh, lont[0]) + dot(ll, lont[0]) + dot(lh, lont[1])
        for lev in range(LEVELS):
            p, at = lev // 2, slice(128 * (lev % 2), 128 * (lev % 2) + 128)
            c3[lev, 0] = c[8 * p : 8 * p + 8, at]
            c3[(lev + YB) % BANDS, 1] = c[8 * p : 8 * p + 8, at]

        @pl.loop(0, BANDS - 1)
        def _(i):
            b = band_peer(i)
            push(c3.at[b], r3.at[me_b], 14, on_band(b))

        r3[me_b] = c3[me_b]

    def gather_in():
        wait_for(r3.at[pl.ds(0, BANDS - 1)], recv.at[14])
        group = lax.broadcasted_iota(jnp.int32, (BANDS, 8, 128), 2) // 32
        both = []
        for s in range(2):
            r = r3[:, s]
            e = jnp.stack([jnp.where(group == j, r, 0.0) for j in range(4)], axis=1)
            both.append(e.reshape(512, 128))
        eh, el = split(jnp.concatenate(both, axis=1))
        oh, ol = split(dot(selt[...], eh) + dot(selt[...], el))
        for s in range(2):
            at = slice(128 * s, 128 * s + 128)
            ct[s] = dot_t(fold[...], oh[:, at]) + dot_t(fold[...], ol[:, at])
        push(ct.at[:, pl.ds(0, 8)], hl.at[1], 15, on_member(west))
        push(ct.at[:, pl.ds(24, 8)], hl.at[0], 16, on_member(east))

    def spread_b():
        wait_for(hl.at[1], recv.at[15])
        wait_for(hl.at[0], recv.at[16])
        own_part = ct[:, pl.ds(8, LON)] + jnp.concatenate([hl[0], hl[1]], axis=1)
        g4[zl] = own_part * SCALE

        @pl.loop(1, ZL)
        def _(d):
            push(g4.at[zl], g4.at[zl], 17, on_member(zl_peer(d)))

    def spread_a():
        wait_for(g4.at[pl.ds(0, ZL - 1)], recv.at[17])
        for s in range(2):

            @pl.loop(1, XC // 2)
            def _(d):
                push(g4.at[:, s], cgt.at[s, core, xx], 18 + s, on_member(x_peer(d)))

            cgt[s, core, xx] = g4[:, s]

    def spread_core(s):
        wait_for(cgt.at[s, 0, pl.ds(0, XC // 2 - 1)], recv.at[18 + s])
        push(cgt.at[s, core], cgt.at[s, core], 24 + s, on_member(other))

    def weigh(s):
        wait_for(cgt.at[s, 0], recv.at[24 + s])
        for i in range(ZL):
            at = pl.ds(128 * i, 128)
            g = jnp.concatenate(
                [cgt[s, c, x, i] for x in range(XC // 2) for c in range(2)], axis=0
            ).T
            for k in range(2):
                w = gm[s, k, :, at] * g
                h = w.astype(BF16)
                wsc[s, 0, k, :, at] = h
                wsc[s, 1, k, :, at] = (w - h.astype(F32)).astype(BF16)

    def adjoint(s, half, k):
        rows = pl.ds(BLOCK * half, BLOCK)
        ph, plo = atph[s, rows], atpl[s, rows]
        t = dot(ph, wsc[s, 0, k]) + dot(plo, wsc[s, 0, k]) + dot(ph, wsc[s, 1, k])
        th, tl = split(t)
        gb[s, k, rows] = dot(th, bh[...]) + dot(tl, bh[...]) + dot(th, bl[...])

    def give(s, half, k):
        to = (behind, ahead)[s] if half else beside

        @pl.loop(0 if half else 1, YB)
        def _(y):
            rows = pl.ds(pl.multiple_of(BLOCK * half + LAT * lax.rem(yb + y, YB), LAT), LAT)
            push(gb.at[s, k, rows], ob.at[k, level[s]], 20 + s, on_band(to(y)))

        if not half:
            ob[k, level[s]] = gb[s, k, mine, :]

    def finish():
        for s in range(2):
            wait_for(seven, recv.at[20 + s])
        out[...] = ob[...] + cv[...]
        for ph in (0, 1, 4, 5, 20, 21):
            wait_for(seven, send.at[ph])
        for ph in (2, 3, 6, 7):
            wait_for(two, send.at[ph])
        for s in range(2):
            wait_for(pc.at[s], send.at[22 + s])
            wait_for(pc.at[s], send.at[24 + s])
            wait_for(pa.at[s, pl.ds(0, XC // 2 - 1)], send.at[8 + s])
            wait_for(pa.at[s, pl.ds(0, XC // 2 - 1)], send.at[18 + s])
        wait_for(pb.at[pl.ds(0, ZL - 1)], send.at[10])
        wait_for(pb.at[pl.ds(0, ZL - 1)], send.at[17])
        for ph in (11, 12, 15, 16):
            wait_for(hl.at[0], send.at[ph])
        wait_for(r2.at[pl.ds(0, BANDS - 1)], send.at[13])
        wait_for(r3.at[pl.ds(0, BANDS - 1)], send.at[14])

    relay()
    prepare()
    fields()
    products(0)
    products(1)
    reduce_a(0)
    reduce_a(1)
    reduce_b()
    halo()
    hand_out()
    fine()
    gather_in()
    spread_b()
    spread_a()
    spread_core(0)
    spread_core(1)
    weigh(0)
    adjoint(0, 1, 0)
    give(0, 1, 0)
    weigh(1)
    for s, half, k in ((1, 1, 0), (0, 1, 1), (1, 1, 1), (0, 0, 0), (1, 0, 0), (0, 0, 1), (1, 0, 1)):
        adjoint(s, half, k)
        give(s, half, k)
    finish()


def body(controls, members, loc_lon, loc_lat, balance, innovation, obs_weight):
    consts = constants()
    hbm = pl.BlockSpec(memory_space=pl.ANY)
    vmem = pl.BlockSpec(memory_space=pltpu.VMEM)
    f32 = lambda *s: pltpu.VMEM(s, F32)
    b16 = lambda *s: pltpu.VMEM(s, BF16)
    small = (loc_lon, loc_lat, balance, innovation, obs_weight)
    return pl.pallas_call(
        kernel,
        out_shape=jax.ShapeDtypeStruct(controls.shape, F32),
        in_specs=[hbm] * (7 + len(consts)),
        out_specs=vmem,
        scratch_shapes=[pltpu.VMEM(v.shape, v.dtype) for v in (*small, *consts)]
        + [
            f32(2, 2, 2 * BLOCK, NXC),
            f32(2, 2, NYC, NXC),
            f32(2, 2, NYC, NXC),
            f32(2, ZL, XC // 2, 2, LON, NYC),
            f32(2, ZL, XC // 2, LON, NYC),
            f32(2, XC // 2, ZL, LON, NYC),
            f32(2, XC // 2, ZL, LON, NYC),
            f32(ZL, 2, LON, NYC),
            f32(ZL, 2, LON, NYC),
            f32(2, 32, NYC),
            f32(BANDS, 2, 8, 128),
            f32(BANDS, 2, 8, 128),
            f32(3, 32, LEVELS * 64),
            f32(BANDS, 2, 8, 128),
            f32(BANDS, 2, 8, 128),
            f32(2, 32, NYC),
            f32(2, 2, 8, NYC),
            f32(ZL, 2, LON, NYC),
            f32(2, 2, XC // 2, ZL, LON, NYC),
            f32(2, 2, 2 * BLOCK, NXC),
            b16(2, 2, 2, NYC, NXC),
            pltpu.VMEM(controls.shape, F32),
            pltpu.VMEM(controls.shape, F32),
            b16(NXC, NXC), b16(NXC, NXC), f32(NYC, NYC),
            b16(2, NYC, 6 * BLOCK), b16(2, 2 * BLOCK, NYC), b16(2, 2 * BLOCK, NYC),
            f32(5, 64, 128), f32(LEVELS // 2, 64, 128), f32(LEVELS // 2, 64, 128),
            pltpu.SemaphoreType.DMA((26,)),
            pltpu.SemaphoreType.DMA((26,)),
            pltpu.SemaphoreType.DMA((2, 2)),
            pltpu.SemaphoreType.DMA((14,)),
            pltpu.SemaphoreType.REGULAR,
        ],
        compiler_params=pltpu.CompilerParams(
            collective_id=0, has_side_effects=True, vmem_limit_bytes=46 << 20
        ),
        name="gradient",
    )(controls, members, *small, *consts)


def solution(mesh):
    return jax.shard_map(
        body,
        mesh=mesh,
        in_specs=(
            P("member", None, "band", None),
            P("member", None, "band", None),
            P(),
            P(),
            P(None, "band", "member"),
            P(None, "band", "member"),
            P(None, "band", "member"),
        ),
        out_specs=P("member", None, "band", None),
        check_vma=False,
    )
```
